256 devices in a mesh: ctx: 64 (over x, z, core), tp: 4 (over y).
Axes of the slice: x: 4, y: 4, z: 8, core: 2. Of those that a mesh axis runs over, the one named last changes fastest.
Arguments:
- layer_input: bfloat16 [8192, 4096], P(('ctx', 'tp')), may hold values from -8 to 8
- dt_weight: bfloat16 [4096, 128], P(None, 'tp'), may hold values from -1 to 1
- dt_bias: float32 [128], P('tp'), may hold values from -5.5 to -4.5
- a_log: float32 [128], P('tp'), may hold values from -4.5 to 1.5
- ssm_input: bfloat16 [8192, 8192], P('ctx', 'tp'), may hold values from -6 to 6
- b_in: bfloat16 [8192, 1024], P('ctx', 'tp'), may hold values from -6 to 6
- c_in: bfloat16 [8192, 1024], P('ctx', 'tp'), may hold values from -6 to 6
- out_grad: bfloat16 [8192, 8192], P('ctx', 'tp'), may hold values from -3 to 3
Outputs:
- grad_ssm_input: bfloat16 [8192, 8192], P('ctx', 'tp')
- grad_b_in: bfloat16 [8192, 1024], P('ctx', 'tp')
- grad_c_in: bfloat16 [8192, 1024], P('ctx', 'tp')
- grad_layer_input: bfloat16 [8192, 4096], P(('ctx', 'tp'))
- grad_dt_weight: float32 [4096, 128], P(None, 'tp')
- grad_dt_bias: float32 [128], P('tp')
- grad_a_log: float32 [128], P('tp')
The draws below stay inside these ranges and needn't reach their ends.
All inputs are finite; a program needn't handle non-finite values.
Results may differ from the reference program's by a relative error of at most 0.0095.
Values may be sent and summed in bfloat16 or wider, within the bound.
No kernel may reach another device: no remote copies, remote signals or barrier semaphores. Data moves between devices by JAX's collectives and lax.ppermute only.
A program may use at most 320 MiB of HBM per device.

```python
import math
import jax
import jax.numpy as jnp
from jax import lax

D = 4096
HEADS = 128
HEAD_DIM = 64
STATE = 128
GROUPS = 8
SPAN = 128
TOK_DEV = 128
SEQUENCE_TOKENS = 8192


def common_direction(key):
    value_entries = jax.random.normal(jax.random.fold_in(key, 11), (D,), jnp.float32)
    return jnp.clip(value_entries, -4.0, 4.0)


def draw_layer_input(key, part):
    probe_direction = common_direction(key)
    key = jax.random.fold_in(key, 1)
    jitter_random_key, magnitude_random_key, spike_random_key = jax.random.split(key, 3)
    baseline_share = jax.random.normal(jitter_random_key, (SEQUENCE_TOKENS, D), jnp.float32)
    blocks = SEQUENCE_TOKENS // TOK_DEV
    block_scale = jnp.exp(jax.random.uniform(magnitude_random_key, (blocks,), jnp.float32, -0.7, 0.7))
    per_row_scale = jnp.repeat(block_scale, TOK_DEV, total_repeat_length=SEQUENCE_TOKENS)
    spike_row_picks = jax.random.randint(spike_random_key, (3,), 0, SEQUENCE_TOKENS)
    token_positions = jnp.arange(SEQUENCE_TOKENS, dtype=jnp.int32)
    spike_row_mask = jnp.any(token_positions[:, None] == spike_row_picks[None, :], axis=1).astype(jnp.float32)
    value_entries = baseline_share * per_row_scale[:, None] + 0.34 * spike_row_mask[:, None] * probe_direction[None, :]
    return jnp.clip(value_entries, -8.0, 8.0).astype(jnp.bfloat16)


def draw_dt_weight(key, part):
    probe_direction = common_direction(key)
    key = jax.random.fold_in(key, 2)
    noise_part = jnp.clip(jax.random.normal(key, (D, HEADS), jnp.float32), -4.0, 4.0)
    value_entries = 0.25 * noise_part * D ** (-0.5) + 8.0 * probe_direction[:, None] / D
    return jnp.clip(value_entries, -1.0, 1.0).astype(jnp.bfloat16)


def draw_a_log(key, part):
    key = jax.random.fold_in(key, 3)
    pick_key, slow_key, quick_key = jax.random.split(key, 3)
    fast_share = 0.5
    fast_mask = jax.random.uniform(pick_key, (HEADS,), jnp.float32) < fast_share
    slow_top = max(-4.2, math.log(1.2) - math.log(0.01 * SEQUENCE_TOKENS))
    slow_rate = jax.random.uniform(slow_key, (HEADS,), jnp.float32, -4.5, slow_top)
    quick_rate = jax.random.uniform(quick_key, (HEADS,), jnp.float32, math.log(0.5), math.log(0.7))
    return jnp.where(fast_mask, quick_rate, slow_rate)


def level_of(stream_key, dims, cuts, low, largest):
    gain = 1.0
    for position, blocks in cuts:
        heights = jax.random.uniform(jax.random.fold_in(jax.random.fold_in(stream_key, 6), position), (blocks,), jnp.float32, low / len(cuts), largest / len(cuts))
        gain = gain * jnp.repeat(jnp.exp(heights), dims[position] // blocks).reshape((-1,) + (1,) * (len(dims) - 1 - position))
    return gain


def scatter_about(stream_key, shape, scale, reach, shards=(), kind=jnp.bfloat16):
    entries = scale * jax.random.normal(stream_key, shape, jnp.float32)
    if shards:
        entries = entries * level_of(stream_key, shape, shards, -0.22, 0.18)
    return jnp.clip(entries, -reach, reach).astype(kind)


def setup_inputs(seed: int = 0) -> dict:
    streams_of = jax.random.split(jax.random.key(seed), 9)
    layer_input = draw_layer_input(jax.random.fold_in(streams_of[8], 71), 0)
    dt_weight = draw_dt_weight(jax.random.fold_in(streams_of[8], 71), 0)
    dt_bias = jnp.clip(-5.5 + 1.0 * jax.random.uniform(streams_of[2], (HEADS,), jnp.float32) ** level_of(streams_of[2], (HEADS,), ((0, 4),), -0.2, 0.2), -5.5, -4.5)
    a_log = draw_a_log(jax.random.fold_in(streams_of[8], 71), 0)
    ssm_input = scatter_about(streams_of[4], (SEQUENCE_TOKENS, HEADS * HEAD_DIM), 1.0, 6.0, ((0, 64), (1, 4)))
    b_in = scatter_about(streams_of[5], (SEQUENCE_TOKENS, GROUPS * STATE), 1.0, 6.0, ((0, 64), (1, 4)))
    c_in = scatter_about(streams_of[6], (SEQUENCE_TOKENS, GROUPS * STATE), 1.0, 6.0, ((0, 64), (1, 4)))
    out_grad = scatter_about(streams_of[7], (SEQUENCE_TOKENS, HEADS * HEAD_DIM), 0.5, 3.0, ((0, 64), (1, 4)))
    return dict(layer_input=layer_input, dt_weight=dt_weight, dt_bias=dt_bias, a_log=a_log, ssm_input=ssm_input, b_in=b_in, c_in=c_in, out_grad=out_grad)


HIGHEST = lax.Precision.HIGHEST


def product(form, left, right):
    return jnp.einsum(form, left.astype(jnp.float32), right.astype(jnp.float32), precision=HIGHEST)


def span_operands(inputs, grad_out, step_block, log_cum):
    final_cum = log_cum[..., -1:, :, :]
    remain = jnp.exp(final_cum - log_cum)
    growth = jnp.exp(log_cum)
    scaled = step_block[..., None] * inputs.astype(jnp.float32)
    in_weighted = (remain[..., None] * scaled).astype(jnp.bfloat16)
    out_weighted = (growth[..., None] * grad_out.astype(jnp.float32)).astype(jnp.bfloat16)
    return scaled, in_weighted, out_weighted


def span_grads(inputs, grad_out, b_block, c_block, step_block, log_cum, scaled, in_weighted, out_weighted, start_state, end_cot):
    length = log_cum.shape[0]
    grads_f = grad_out.astype(jnp.float32)
    scaled_bf = scaled.astype(jnp.bfloat16)
    start_bf = start_state.astype(jnp.bfloat16)
    end_bf = end_cot.astype(jnp.bfloat16)
    scores = product("tgn,sgn->gts", c_block, b_block)
    cum_heads = jnp.transpose(log_cum, (1, 2, 0))
    row_ids = lax.broadcasted_iota(jnp.int32, (length, length), 0)
    col_ids = lax.broadcasted_iota(jnp.int32, (length, length), 1)
    lower_mask = row_ids >= col_ids
    spread = jnp.minimum(cum_heads[..., :, None] - cum_heads[..., None, :], 0.0)
    decay_mat = jnp.where(lower_mask, jnp.exp(spread), 0.0)
    mixing = scores[:, None] * decay_mat
    mixing_bf = mixing.astype(jnp.bfloat16)
    grad_mixing = product("tghp,sghp->ghts", grad_out, scaled_bf)
    grad_scores = jnp.sum(grad_mixing * decay_mat, axis=1).astype(jnp.bfloat16)
    pulled = product("ghpn,sgn->sghp", end_bf, b_block)
    from_state = product("ghpn,tgn->tghp", start_bf, c_block)
    final_cum = log_cum[length - 1]
    remain = jnp.exp(final_cum[None] - log_cum)
    growth = jnp.exp(log_cum)
    grad_scaled = product("ghts,tghp->sghp", mixing_bf, grad_out) + remain[..., None] * pulled
    grad_b = product("gts,tgn->sgn", grad_scores, c_block) + product("sghp,ghpn->sgn", in_weighted, end_bf)
    grad_c = product("gts,sgn->tgn", grad_scores, b_block) + product("tghp,ghpn->tgn", out_weighted, start_bf)
    weighted = grad_mixing * mixing
    grad_cum = jnp.transpose(jnp.sum(weighted, axis=3) - jnp.sum(weighted, axis=2), (2, 0, 1))
    grad_cum = grad_cum + growth * jnp.sum(grads_f * from_state, axis=3)
    touched = remain * jnp.sum(scaled * pulled, axis=3)
    last_term = jnp.sum(touched, axis=0) + jnp.exp(final_cum) * jnp.sum(end_cot * start_state, axis=(2, 3))
    grad_cum = grad_cum - touched
    grad_cum = grad_cum.at[length - 1].add(last_term)
    grad_log = jnp.cumsum(grad_cum[::-1], axis=0)[::-1]
    grad_x = step_block[..., None] * grad_scaled
    grad_step = jnp.sum(inputs.astype(jnp.float32) * grad_scaled, axis=3)
    return grad_x, grad_b, grad_c, grad_step, grad_log


def reference(layer_input, dt_weight, dt_bias, a_log, ssm_input, b_in, c_in, out_grad):
    projected = jnp.dot(layer_input, dt_weight, preferred_element_type=jnp.float32)
    pre_step = projected + dt_bias[None, :]
    step_size = jax.nn.softplus(pre_step)
    decay_rate = jnp.exp(a_log)
    span_count = SEQUENCE_TOKENS // SPAN
    per_group = HEADS // GROUPS
    block_shape = (span_count, SPAN, GROUPS, per_group)
    step_all = step_size.reshape(block_shape)
    cum_all = jnp.cumsum(((-decay_rate)[None, :] * step_size).reshape(block_shape), axis=1)
    input_blocks = ssm_input.reshape(span_count, SPAN, GROUPS, per_group * HEAD_DIM)
    grad_blocks = out_grad.reshape(span_count, SPAN, GROUPS, per_group * HEAD_DIM)
    b_blocks = b_in.reshape(span_count, SPAN, GROUPS, STATE)
    c_blocks = c_in.reshape(span_count, SPAN, GROUPS, STATE)

    def one_group(group_index):
        def select_group(value_entries):
            return lax.dynamic_slice_in_dim(value_entries, group_index, 1, 2)

        inputs_g = select_group(input_blocks).reshape(span_count, SPAN, 1, per_group, HEAD_DIM)
        grads_g = select_group(grad_blocks).reshape(span_count, SPAN, 1, per_group, HEAD_DIM)
        b_group = select_group(b_blocks)
        c_group = select_group(c_blocks)
        step_group = select_group(step_all)
        cum_group = select_group(cum_all)
        zero_state = jnp.zeros((1, per_group, HEAD_DIM, STATE), jnp.float32)

        def backward_chain(carried, block_item):
            grad_out, c_block, log_cum = block_item
            growth = jnp.exp(log_cum)
            out_weighted = (growth[..., None] * grad_out.astype(jnp.float32)).astype(jnp.bfloat16)
            block_decay = jnp.exp(log_cum[SPAN - 1])
            renewed = block_decay[:, :, None, None] * carried + product("tghp,tgn->ghpn", out_weighted, c_block)
            return renewed, carried

        _, end_cots = lax.scan(backward_chain, zero_state, (grads_g, c_group, cum_group), reverse=True)

        def forward_chain(carried, block_item):
            inputs, b_block, c_block, grad_out, step_block, log_cum, end_cot = block_item
            scaled, in_weighted, out_weighted = span_operands(inputs, grad_out, step_block, log_cum)
            block_decay = jnp.exp(log_cum[SPAN - 1])
            outcome = span_grads(inputs, grad_out, b_block, c_block, step_block, log_cum, scaled, in_weighted, out_weighted, carried, end_cot)
            renewed = block_decay[:, :, None, None] * carried + product("sghp,sgn->ghpn", in_weighted, b_block)
            return renewed, outcome

        _, results = lax.scan(forward_chain, zero_state, (inputs_g, b_group, c_group, grads_g, step_group, cum_group, end_cots))
        return (results[0].astype(jnp.bfloat16), results[1].astype(jnp.bfloat16), results[2].astype(jnp.bfloat16), results[3], results[4])

    grads = lax.map(one_group, jnp.arange(GROUPS, dtype=jnp.int32))
    grad_ssm_input = jnp.transpose(grads[0], (1, 2, 0, 3, 4, 5)).reshape(SEQUENCE_TOKENS, HEADS * HEAD_DIM)
    grad_b_in = jnp.transpose(grads[1], (1, 2, 0, 3, 4)).reshape(SEQUENCE_TOKENS, GROUPS * STATE)
    grad_c_in = jnp.transpose(grads[2], (1, 2, 0, 3, 4)).reshape(SEQUENCE_TOKENS, GROUPS * STATE)
    step_local = jnp.transpose(grads[3], (1, 2, 0, 3, 4)).reshape(SEQUENCE_TOKENS, HEADS)
    grad_log = jnp.transpose(grads[4], (1, 2, 0, 3, 4)).reshape(SEQUENCE_TOKENS, HEADS)
    grad_step = step_local - decay_rate[None, :] * grad_log
    grad_a_log = decay_rate * (-jnp.sum(grad_log * step_size, axis=0))
    grad_pre = grad_step * jax.nn.sigmoid(pre_step)
    zed_grad = grad_pre.astype(jnp.bfloat16)
    grad_dt_bias = jnp.sum(grad_pre, axis=0)
    grad_dt_weight = jnp.dot(layer_input.T, zed_grad, preferred_element_type=jnp.float32)
    grad_layer_input = jnp.dot(zed_grad, dt_weight.T, preferred_element_type=jnp.float32).astype(jnp.bfloat16)
    return (grad_ssm_input, grad_b_in, grad_c_in, grad_layer_input, grad_dt_weight, grad_dt_bias, grad_a_log)
```

```python
import jax
import jax.numpy as jnp
from jax import lax
from jax.experimental import pallas as pl
from jax.experimental.pallas import tpu as pltpu
from jax.sharding import Mesh
from jax.sharding import PartitionSpec as P

BF = jnp.bfloat16
F32 = jnp.float32
CHIPS, CORES, TP = 32, 2, 4
SPAN = 128
N = 128
HD = 64
HH = 16
W = HH * HD
D = 4096
PIECE = 32


def dot(a, b):
    return lax.dot_general(a, b, (((1,), (0,)), ((), ())), preferred_element_type=F32)


def dot_nt(a, b):
    return lax.dot_general(a, b, (((1,), (1,)), ((), ())), preferred_element_type=F32)


def split3(v):
    hi = v.astype(BF).astype(F32)
    rest = v - hi
    mid = rest.astype(BF).astype(F32)
    return [hi, mid, rest - mid]


def iota(shape, dim):
    return lax.broadcasted_iota(jnp.int32, shape, dim)


def triangle(keep):
    return jnp.where(keep(iota((SPAN, SPAN), 0), iota((SPAN, SPAN), 1)), 1.0, 0.0).astype(BF)


def sum_by(rows, matrix):
    r = rows.shape[0]
    out = dot(jnp.concatenate(split3(rows), 0).astype(BF), matrix)
    return out[:r] + out[r : 2 * r] + out[2 * r :]


def columns(first, second):
    stack = split3(first) + split3(second) + [jnp.zeros((32, SPAN), F32)]
    return jnp.concatenate(stack, 0).T.astype(BF)


def spread_maps():
    row = lax.broadcasted_iota(jnp.int32, (128, 2 * W), 0)
    col = lax.broadcasted_iota(jnp.int32, (128, 2 * W), 1)
    part = row // 48
    same = (row % 16) == (col % W) // HD
    return jnp.where(same & (part == col // W), 1.0, 0.0).astype(BF)


def project_kernel(scal, w, l0, l1, l2, l3, own, other):
    rows = jnp.concatenate([l0[...], l1[...], l2[...], l3[...]], 0)
    acc = pltpu.roll(dot_nt(w[...], rows), scal[0], 1)
    own[...] = acc[:HH]
    other[...] = acc[HH:]


def state_kernel(
    scal, po, pp, bias, alog, xo, xp, yo, yp, bo, bp, co, cp, maps,
    msg, s_first, p_second, small, decay,
    s_all, p_all,
):
    pre = jnp.concatenate([po[...] + bias[...], pp[...] + bias[...]], 0)
    step = jnp.maximum(pre, 0.0) + jnp.log1p(jnp.exp(-jnp.abs(pre)))
    rate = jnp.exp(alog[...])
    rate = jnp.concatenate([rate, rate], 0)
    cum = sum_by(-rate * step, triangle(lambda u, t: u <= t))
    small[0] = pre
    small[1] = step
    small[2] = cum
    remain_step = jnp.exp(cum[:, SPAN - 1 :] - cum) * step
    growth = jnp.exp(cum)
    for b, (x, y, bm, cm) in enumerate(((xo, yo, bo, co), (xp, yp, bp, cp))):
        rows = slice(b * HH, (b + 1) * HH)
        weights = columns(remain_step[rows], growth[rows])
        b_t = bm[...].astype(F32).T.astype(BF)
        c_t = cm[...].astype(F32).T.astype(BF)
        for k in range(W // 256):
            cols = slice(k * 256, (k + 1) * 256)
            w_in = dot(weights, maps[:, cols])
            s_all[b, :, cols] = dot(b_t, (w_in * x[:, cols].astype(F32)).astype(BF))
            w_out = dot(weights, maps[:, W + k * 256 : W + (k + 1) * 256])
            p_all[b, :, cols] = dot(c_t, (w_out * y[:, cols].astype(F32)).astype(BF))
            decay[b, :, cols] = jnp.broadcast_to(w_out[SPAN - 1 :], (8, 256))
    first = scal[1]
    second = 1 - first
    for k in range(W // 128):
        cols = slice(k * 128, (k + 1) * 128)
        d_first, d_second = decay[first, 0:1, cols], decay[second, 0:1, cols]
        s_f, p_s = s_all[first, :, cols], p_all[second, :, cols]
        forward = (d_second * s_f + s_all[second, :, cols]).astype(BF)
        backward = (p_all[first, :, cols] + d_first * p_s).astype(BF)
        s_first[:, cols] = s_f.astype(BF)
        p_second[:, cols] = p_s.astype(BF)
        d3 = jnp.concatenate(split3(d_first * d_second) + [jnp.zeros((13, 128), F32)], 0).astype(BF)
        for r in range(N // PIECE):
            at = k * (N // PIECE) + r
            msg[at, 0:PIECE, :] = forward[r * PIECE : (r + 1) * PIECE]
            msg[at, PIECE : 2 * PIECE, :] = backward[r * PIECE : (r + 1) * PIECE]
            msg[at, 2 * PIECE : 2 * PIECE + 16, :] = d3


def fold_kernel(msg, out):
    decays = []
    for k in range(CHIPS):
        d = msg[k, 2 * PIECE : 2 * PIECE + 16, :].astype(F32)
        decays.append(d[0:1] + d[1:2] + d[2:3])
    total = jnp.zeros((PIECE, 128), F32)
    for k in range(CHIPS):
        out[k, 0:PIECE, :] = total.astype(BF)
        total = total * decays[k] + msg[k, 0:PIECE, :].astype(F32)
    total = jnp.zeros((PIECE, 128), F32)
    for k in reversed(range(CHIPS)):
        out[k, PIECE : 2 * PIECE, :] = total.astype(BF)
        total = total * decays[k] + msg[k, PIECE : 2 * PIECE, :].astype(F32)


def intra_kernel(small, xo, xp, yo, yp, bo, bp, co, cp, gs, gb, gc, rows_out, cols_out):
    lane = iota((SPAN, 128), 1)
    low = lane < HD
    later = lane >= iota((SPAN, SPAN), 0)
    step_t = jnp.concatenate([small[1], jnp.zeros((96, 128), F32)], 0).T
    cum_t = jnp.concatenate([small[2], jnp.zeros((96, 128), F32)], 0).T
    sums = jnp.zeros((SPAN, 128), F32)
    zero = jnp.zeros((SPAN, 128), BF)
    for b, (x, y, bm, cm) in enumerate(((xo, yo, bo, co), (xp, yp, bp, cp))):
        scores = dot_nt(bm[...], cm[...])
        grad_scores = jnp.zeros((SPAN, SPAN), F32)
        for pair in range(HH // 2):
            cols = slice(pair * 128, (pair + 1) * 128)
            xs, ys = x[:, cols], y[:, cols]
            halves = []
            for side in range(2):
                h = b * HH + pair * 2 + side
                mine = jnp.where(low if side == 0 else ~low, xs, zero)
                grad_mixing = dot_nt(mine, ys)
                spread = small[2, h : h + 1, :] - cum_t[:, h : h + 1]
                decay = jnp.where(later, jnp.exp(jnp.minimum(spread, 0.0)), 0.0)
                mixing = scores * decay
                halves.append(dot(mixing.astype(BF), ys))
                scaled = grad_mixing * step_t[:, h : h + 1]
                grad_scores = grad_scores + scaled * decay
                rows_out[h : h + 1, :] = jnp.sum(scaled * mixing, axis=0, keepdims=True)
                col = jnp.sum(grad_mixing * mixing, axis=1, keepdims=True)
                sums = jnp.where(lane == h, col, sums)
            gs[b, :, cols] = jnp.where(low, halves[0], halves[1])
        gs_bf = grad_scores.astype(BF)
        gb[b] = dot(gs_bf, cm[...])
        gc[b] = dot(grad_scores.T.astype(BF), bm[...])
    cols_out[...] = sums.T[: 2 * HH]


def assemble(scal, got, s_first, p_second, decay, start, end, exact):
    first = scal[1]
    second = 1 - first
    for k in range(W // 128):
        cols = slice(k * 128, (k + 1) * 128)
        d_first, d_second = decay[first, 0:1, cols], decay[second, 0:1, cols]
        for r in range(N // PIECE):
            at = k * (N // PIECE) + r
            rows = slice(r * PIECE, (r + 1) * PIECE)
            s_in, e_in = got[at, 0:PIECE, :], got[at, PIECE : 2 * PIECE, :]
            start[first, rows, cols] = s_in
            end[second, rows, cols] = e_in
            s_f, e_f = s_in.astype(F32), e_in.astype(F32)
            s_next = d_first * s_f + s_first[rows, cols].astype(F32)
            e_next = d_second * e_f + p_second[rows, cols].astype(F32)
            start[second, rows, cols] = s_next.astype(BF)
            end[first, rows, cols] = e_next.astype(BF)
            if exact is not None:
                one = jnp.sum(s_f * e_next, axis=0, keepdims=True)
                two = jnp.sum(s_next * e_f, axis=0, keepdims=True)
                if r == 0:
                    sum_one, sum_two = one, two
                else:
                    sum_one, sum_two = sum_one + one, sum_two + two
        if exact is not None:
            exact[first, 0:1, cols] = sum_one
            exact[second, 0:1, cols] = sum_two


def head_map(shape, head_dim, chan_dim):
    return jnp.where(iota(shape, chan_dim) // HD == iota(shape, head_dim), 1.0, 0.0).astype(BF)


def pre_kernel(
    scal, got, s_first, p_second, decay, small, rows_in, cols_in, alog,
    xo, xp, yo, yp, bo, bp, co, cp, lo, lp,
    zed_out, msg,
    start, end, exact,
):
    assemble(scal, got, s_first, p_second, decay, start, end, exact)
    by_head = head_map((W, 128), 1, 0)
    sums = []
    joint = []
    for b, (x, y, bm, cm) in enumerate(((xo, yo, bo, co), (xp, yp, bp, cp))):
        for grad, mat, state in ((x, bm, end), (y, cm, start)):
            total = jnp.zeros((SPAN, 128), F32)
            for k in range(W // 256):
                cols = slice(k * 256, (k + 1) * 256)
                prod = dot(mat[...], state[b, :, cols]) * grad[:, cols].astype(F32)
                hi = prod.astype(BF)
                lo_part = (prod - hi.astype(F32)).astype(BF)
                total = total + dot(hi, by_head[cols]) + dot(lo_part, by_head[cols])
            sums.append(total.T[:HH])
        rows8 = jnp.concatenate(split3(exact[b, 0:1, :]) + [jnp.zeros((5, W), F32)], 0).astype(BF)
        joint.append(jnp.sum(dot_nt(head_map((HH, W), 0, 1), rows8), axis=1, keepdims=True))
    x_pulled = jnp.concatenate([sums[0], sums[2]], 0)
    y_state = jnp.concatenate([sums[1], sums[3]], 0)
    joint = jnp.concatenate(joint, 0)
    pre, step, cum = small[0], small[1], small[2]
    last = cum[:, SPAN - 1 :]
    rate = jnp.exp(alog[...])
    rate = jnp.concatenate([rate, rate], 0)
    q = jnp.exp(last - cum) * x_pulled
    cols = cols_in[...]
    u = rows_in[...] - step * cols + jnp.exp(cum) * y_state
    grad_log = (
        sum_by(u, triangle(lambda u, t: u >= t))
        + sum_by(step * q, triangle(lambda u, t: u < t))
        + jnp.exp(last) * joint
    )
    grad_step = cols + q - rate * grad_log
    grad_pre = grad_step * jax.nn.sigmoid(pre)
    for b in range(2):
        where = scal[1] if b == 0 else 1 - scal[1]
        zed_out[where] = grad_pre[b * HH : (b + 1) * HH].astype(BF)
    rolled = pltpu.roll(grad_pre, scal[2], 1).astype(BF)
    diagonal = iota((HH, 128), 0) == iota((HH, 128), 1)

    def as_row(v):
        v = v[:HH] + v[HH:]
        v = jnp.sum(v, axis=1, keepdims=True)
        return jnp.sum(jnp.where(diagonal, v, 0.0), axis=0, keepdims=True)

    extra = split3(as_row(grad_pre)) + split3(as_row(-grad_log * step))
    extra = jnp.concatenate(extra + [jnp.zeros((10, 128), F32)], 0).astype(BF)
    for k in range(D // 256):
        cols = slice(k * 256, (k + 1) * 256)
        part = dot(rolled[:HH], lo[:, cols]) + dot(rolled[HH:], lp[:, cols])
        for j in range(2):
            msg[2 * k + j, 0:HH, :] = part[:, j * 128 : (j + 1) * 128].astype(BF)
            msg[2 * k + j, HH : 2 * HH, :] = extra


def sum_kernel(msg, out, totals):
    total = jnp.zeros((2 * HH, 128), F32)
    for k in range(CHIPS):
        total = total + msg[k].astype(F32)
    rounded = total[:HH].astype(BF)
    for k in range(CHIPS):
        out[k] = rounded
    e = total[HH:]
    bias = e[0:1] + e[1:2] + e[2:3]
    rate = e[3:4] + e[4:5] + e[5:6]
    totals[...] = jnp.concatenate([bias, rate, jnp.zeros((6, 128), F32)], 0)


def grads_kernel(
    scal, got, s_first, p_second, decay, small, gs, gb, gc, maps,
    xo, xp, yo, yp, bo, bp, co, cp,
    gx_out, gb_out, gc_out,
    start, end,
):
    assemble(scal, got, s_first, p_second, decay, start, end, None)
    step, cum = small[1], small[2]
    remain = jnp.exp(cum[:, SPAN - 1 :] - cum)
    growth = jnp.exp(cum)
    for b, (x, y, bm, cm) in enumerate(((xo, yo, bo, co), (xp, yp, bp, cp))):
        rows = slice(b * HH, (b + 1) * HH)
        w_a = columns(remain[rows], growth[rows])
        w_b = columns(step[rows], step[rows])
        grad_b, grad_c = gb[b], gc[b]
        for k in range(W // 256):
            cols = slice(k * 256, (k + 1) * 256)
            wide = slice(W + k * 256, W + (k + 1) * 256)
            remain_w = dot(w_a, maps[:, cols])
            step_w = dot(w_b, maps[:, cols])
            growth_w = dot(w_a, maps[:, wide])
            pulled = dot(bm[...], end[b, :, cols])
            gx_out[b, :, cols] = (step_w * (gs[b, :, cols] + remain_w * pulled)).astype(BF)
            in_w = (remain_w * (step_w * x[:, cols].astype(F32))).astype(BF)
            out_w = (growth_w * y[:, cols].astype(F32)).astype(BF)
            grad_b = grad_b + dot_nt(in_w, end[b, :, cols])
            grad_c = grad_c + dot_nt(out_w, start[b, :, cols])
        gb_out[b] = grad_b.astype(BF)
        gc_out[b] = grad_c.astype(BF)


def weight_kernel(scal, own, other, out):
    first = scal[1]
    for j in range(CHIPS):
        a, b = own[j].astype(F32), other[j].astype(F32)
        low = jnp.where(first == 0, a, b)
        high = jnp.where(first == 0, b, a)
        out[j * 128 : (j + 1) * 128, :] = jnp.concatenate([low, high], 0).T


def call(kernel, outs, args, scratch=(), flops=0, moved=0, limit=40):
    vmem = pl.BlockSpec(memory_space=pltpu.VMEM)
    specs = [
        pl.BlockSpec(memory_space=pltpu.SMEM) if a.dtype == jnp.int32 else vmem for a in args
    ]
    return pl.pallas_call(
        kernel,
        out_shape=[jax.ShapeDtypeStruct(s, t) for s, t in outs],
        in_specs=specs,
        out_specs=[vmem] * len(outs),
        scratch_shapes=[pltpu.VMEM(s, t) for s, t in scratch],
        compiler_params=pltpu.CompilerParams(vmem_limit_bytes=limit * 2**20),
        cost_estimate=pl.CostEstimate(flops=flops, bytes_accessed=moved, transcendentals=0),
    )(*args)


def swap(v):
    return lax.ppermute(v, "core", [(0, 1), (1, 0)])


def local(layer_input, dt_weight, dt_bias, a_log, ssm_input, b_in, c_in, out_grad):
    core = lax.axis_index("core")
    tp = lax.axis_index("tp")
    scal = jnp.stack([32 * tp, core, (128 - 32 * tp) % 128]).astype(jnp.int32)

    def half(v, which, width, axis):
        return lax.dynamic_slice_in_dim(v, which * width, width, axis)

    pieces = [layer_input] + [
        lax.ppermute(layer_input, "tp", [((i + k) % TP, i) for i in range(TP)]) for k in (1, 3, 2)
    ]
    pieces = [pieces[0], pieces[1], pieces[3], pieces[2]]
    weight_t = dt_weight.T
    weight_mine = jnp.concatenate(
        [half(weight_t, core, HH, 0), half(weight_t, 1 - core, HH, 0)], 0
    )
    operands = []
    for v, width in ((ssm_input, W), (out_grad, W), (b_in, N), (c_in, N)):
        operands += [half(v, core, width, 1), swap(half(v, 1 - core, width, 1))]
    bias = jnp.broadcast_to(half(dt_bias, core, HH, 0)[:, None], (HH, 128))
    alog = jnp.broadcast_to(half(a_log, core, HH, 0)[:, None], (HH, 128))
    maps = spread_maps()

    proj_own, proj_other = call(
        project_kernel, [((HH, 128), F32)] * 2, [scal, weight_mine] + pieces, flops=2**26, moved=2**21
    )
    proj_other = swap(proj_other)
    msg, s_first, p_second, small, decay = call(
        state_kernel,
        [
            ((CHIPS, 2 * PIECE + 16, 128), BF),
            ((N, W), BF),
            ((N, W), BF),
            ((3, 2 * HH, 128), F32),
            ((2, 8, W), F32),
        ],
        [scal, proj_own, proj_other, bias, alog] + operands + [maps],
        [((2, N, W), F32), ((2, N, W), F32)],
        flops=2**28,
        moved=2**22,
    )
    got = lax.all_to_all(msg, "chip", 0, 0, tiled=True)

    weight_t, _ = lax.optimization_barrier((weight_t, small))
    weight_all = lax.all_gather(weight_t, "tp", axis=0, tiled=True)
    rows_own = jnp.concatenate(pieces, 0)
    rows_other = swap(rows_own)
    gs, gb, gc, row_sums, col_sums = call(
        intra_kernel,
        [((2, SPAN, W), F32), ((2, SPAN, N), F32), ((2, SPAN, N), F32)] + [((2 * HH, 128), F32)] * 2,
        [small] + operands,
        flops=2**33,
        moved=2**22,
    )

    (folded,) = call(
        fold_kernel, [((CHIPS, 2 * PIECE, 128), BF)], [got], flops=2**20, moved=2**20
    )
    states = lax.all_to_all(folded, "chip", 0, 0, tiled=True)

    zed, parts = call(
        pre_kernel,
        [((2, HH, 128), BF), ((CHIPS, 2 * HH, 128), BF)],
        [scal, states, s_first, p_second, decay, small, row_sums, col_sums, alog]
        + operands
        + [rows_own, rows_other],
        [((2, N, W), BF), ((2, N, W), BF), ((2, 8, W), F32)],
        flops=2**29,
        moved=2**23,
    )
    shares = lax.all_to_all(parts, "chip", 0, 0, tiled=True)
    zed = jnp.transpose(zed.reshape(CORES, HH, TP, 32), (0, 2, 1, 3)).reshape(CORES * TP, HH, 32)
    zed = lax.all_to_all(zed, ("core", "tp"), 0, 0, tiled=True)
    zed = jnp.transpose(zed.reshape(CORES, TP, HH, 32), (3, 1, 0, 2)).reshape(32, TP * CORES * HH)
    grad_layer_input = dot(zed, weight_all).astype(BF)

    gx, gb, gc = call(
        grads_kernel,
        [((2, SPAN, W), BF), ((2, SPAN, N), BF), ((2, SPAN, N), BF)],
        [scal, states, s_first, p_second, decay, small, gs, gb, gc, maps] + operands,
        [((2, N, W), BF), ((2, N, W), BF)],
        flops=2**32,
        moved=2**23,
    )

    def join(mine, other, axis):
        return jnp.where(
            core == 0,
            jnp.concatenate([mine, other], axis),
            jnp.concatenate([other, mine], axis),
        )

    grad_ssm_input = join(gx[0], swap(gx[1]), 1)
    grad_b_in = join(gb[0], swap(gb[1]), 1)
    grad_c_in = join(gc[0], swap(gc[1]), 1)

    total, totals = call(
        sum_kernel, [((CHIPS, HH, 128), BF), ((8, 128), F32)], [shares], flops=2**20, moved=2**20
    )
    weight_own = lax.all_to_all(total, "chip", 0, 0, tiled=True)
    totals = join(totals[:2, :HH], swap(totals[:2, :HH]), 1)
    grad_dt_bias = totals[0]
    grad_a_log = jnp.exp(a_log) * totals[1]
    (grad_dt_weight,) = call(
        weight_kernel,
        [((D, 2 * HH), F32)],
        [scal, weight_own, swap(weight_own)],
        flops=2**20,
        moved=2**22,
    )
    return (
        grad_ssm_input,
        grad_b_in,
        grad_c_in,
        grad_layer_input,
        grad_dt_weight,
        grad_dt_bias,
        grad_a_log,
    )


def solution(mesh):
    fine = Mesh(mesh.devices.reshape(CHIPS, CORES, TP), ("chip", "core", "tp"))
    ctx = ("chip", "core")
    everything = ("chip", "core", "tp")
    placed = (
        P(everything, None),
        P(None, "tp"),
        P("tp"),
        P("tp"),
        P(ctx, "tp"),
        P(ctx, "tp"),
        P(ctx, "tp"),
        P(ctx, "tp"),
    )
    return jax.shard_map(
        local,
        mesh=fine,
        in_specs=placed,
        out_specs=(
            P(ctx, "tp"),
            P(ctx, "tp"),
            P(ctx, "tp"),
            P(everything, None),
            P(None, "tp"),
            P("tp"),
            P("tp"),
        ),
        check_vma=False,
    )
```

```python
import jax
import jax.numpy as jnp
from jax import lax
from jax.experimental import pallas as pl
from jax.experimental.pallas import tpu as pltpu
from jax.sharding import Mesh
from jax.sharding import PartitionSpec as P

BF = jnp.bfloat16
F32 = jnp.float32
CHIPS, CORES, TP = 32, 2, 4
SPAN = 128
N = 128
HD = 64
HH = 16
W = HH * HD
D = 4096
PIECE = 32


def dot(a, b):
    return lax.dot_general(a, b, (((1,), (0,)), ((), ())), preferred_element_type=F32)


def dot_nt(a, b):
    return lax.dot_general(a, b, (((1,), (1,)), ((), ())), preferred_element_type=F32)


def split3(v):
    hi = v.astype(BF).astype(F32)
    rest = v - hi
    mid = rest.astype(BF).astype(F32)
    return [hi, mid, rest - mid]


def iota(shape, dim):
    return lax.broadcasted_iota(jnp.int32, shape, dim)


def triangle(keep):
    return jnp.where(keep(iota((SPAN, SPAN), 0), iota((SPAN, SPAN), 1)), 1.0, 0.0).astype(BF)


def sum_by(rows, matrix):
    r = rows.shape[0]
    out = dot(jnp.concatenate(split3(rows), 0).astype(BF), matrix)
    return out[:r] + out[r : 2 * r] + out[2 * r :]


def columns(first, second):
    stack = split3(first) + split3(second) + [jnp.zeros((32, SPAN), F32)]
    return jnp.concatenate(stack, 0).T.astype(BF)


def spread_maps():
    row = lax.broadcasted_iota(jnp.int32, (128, 2 * W), 0)
    col = lax.broadcasted_iota(jnp.int32, (128, 2 * W), 1)
    part = row // 48
    same = (row % 16) == (col % W) // HD
    return jnp.where(same & (part == col // W), 1.0, 0.0).astype(BF)


def copy_all(pairs, sems, first=0):
    copies = [pltpu.make_async_copy(a, b, sems.at[first + i]) for i, (a, b) in enumerate(pairs)]
    for c in copies:
        c.start()
    return copies


def wait_all(copies):
    for c in copies:
        c.wait()


def project_kernel(scal, w, bias, l0, l1, l2, l3, own, other, rows_out, sems):
    pieces = (l0, l1, l2, l3)
    copies = copy_all(
        [(v, rows_out.at[pl.ds(32 * k, 32)]) for k, v in enumerate(pieces)], sems
    )
    first = scal[1]
    head = iota((2 * HH, 2 * HH), 0)
    head = jnp.where(first == 0, head, lax.rem(head + HH, 2 * HH))
    mine = iota((2 * HH, 2 * HH), 1) == head
    add = jnp.sum(jnp.where(mine, bias[...], 0.0), axis=1, keepdims=True)
    rows = jnp.concatenate([v[...] for v in pieces], 0)
    acc = pltpu.roll(dot_nt(w[...], rows), scal[0], 1) + add
    own[...] = acc[:HH]
    other[...] = acc[HH:]
    wait_all(copies)


def state_kernel(
    scal, po, pp, alog, xo, xp, yo, yp, bo, bp, co, cp, maps,
    msg_out, keep_out, small_out,
    s_all, p_all, decay, msg, keep, small, sems,
):
    first = scal[1]
    second = 1 - first
    pre = jnp.concatenate([po[...], pp[...]], 0)
    step = jnp.maximum(pre, 0.0) + jnp.log1p(jnp.exp(-jnp.abs(pre)))
    mine = iota((2 * HH, 2 * HH), 1) == lax.rem(iota((2 * HH, 2 * HH), 0), HH) + HH * first
    rate = jnp.exp(jnp.sum(jnp.where(mine, alog[...], 0.0), axis=1, keepdims=True))
    rate = jnp.broadcast_to(rate, (2 * HH, 128))
    cum = sum_by(-rate * step, triangle(lambda u, t: u <= t))
    small[0] = pre
    small[1] = step
    small[2] = cum
    small[3] = rate
    copies = copy_all([(small, small_out)], sems)
    remain_step = jnp.exp(cum[:, SPAN - 1 :] - cum) * step
    growth = jnp.exp(cum)
    for b, (x, y, bm, cm) in enumerate(((xo, yo, bo, co), (xp, yp, bp, cp))):
        rows = slice(b * HH, (b + 1) * HH)
        weights = columns(remain_step[rows], growth[rows])
        b_t = bm[...].astype(F32).T.astype(BF)
        c_t = cm[...].astype(F32).T.astype(BF)
        for k in range(W // 256):
            cols = slice(k * 256, (k + 1) * 256)
            w_in = dot(weights, maps[:, cols])
            s_all[b, :, cols] = dot(b_t, (w_in * x[:, cols].astype(F32)).astype(BF))
            w_out = dot(weights, maps[:, W + k * 256 : W + (k + 1) * 256])
            p_all[b, :, cols] = dot(c_t, (w_out * y[:, cols].astype(F32)).astype(BF))
            decay[b, :, cols] = jnp.broadcast_to(w_out[SPAN - 1 :], (8, 256))
    per = N // PIECE
    for k in range(W // 128):
        cols = slice(k * 128, (k + 1) * 128)
        d_first, d_second = decay[first, 0:1, cols], decay[second, 0:1, cols]
        s_f, p_s = s_all[first, :, cols], p_all[second, :, cols]
        forward = d_second * s_f + s_all[second, :, cols]
        backward = p_all[first, :, cols] + d_first * p_s
        keep[0, :, cols] = s_f.astype(BF)
        keep[1, :, cols] = p_s.astype(BF)
        d3 = split3(d_first * d_second) + [jnp.zeros((5, 128), F32)]
        for r in range(per):
            rows = slice(r * PIECE, (r + 1) * PIECE)
            whole = jnp.concatenate([forward[rows], backward[rows]] + d3, 0)
            msg[k * per + r] = whole.astype(BF)
        if k % 2 == 1:
            done = pl.ds((k - 1) * per, 2 * per)
            copies += copy_all([(msg.at[done], msg_out.at[done])], sems, 1 + k // 2)
    copies += copy_all([(keep, keep_out)], sems, 5)
    wait_all(copies)


def fold_kernel(msg, out):
    parts = [msg[k].astype(F32) for k in range(CHIPS)]
    decays = [v[2 * PIECE : 2 * PIECE + 1] + v[2 * PIECE + 1 : 2 * PIECE + 2] + v[2 * PIECE + 2 : 2 * PIECE + 3] for v in parts]
    total = jnp.zeros((PIECE, 128), F32)
    for k in range(CHIPS):
        out[k, 0:PIECE, :] = total.astype(BF)
        total = total * decays[k] + parts[k][:PIECE]
    total = jnp.zeros((PIECE, 128), F32)
    for k in reversed(range(CHIPS)):
        out[k, PIECE : 2 * PIECE, :] = total.astype(BF)
        total = total * decays[k] + parts[k][PIECE : 2 * PIECE]


def intra_kernel(
    small_in, xo, xp, yo, yp, bo, bp, co, cp, gs, gb, gc, sums_out, small, sums_v, sems
):
    wait_all(copy_all([(small_in, small)], sems))
    lane = iota((SPAN, 128), 1)
    low = lane < HD
    later = lane >= iota((SPAN, SPAN), 0)
    step_t = jnp.concatenate([small[1], jnp.zeros((96, 128), F32)], 0).T
    cum_t = jnp.concatenate([small[2], jnp.zeros((96, 128), F32)], 0).T
    sums = jnp.zeros((SPAN, 128), F32)
    zero = jnp.zeros((SPAN, 128), BF)
    for b, (x, y, bm, cm) in enumerate(((xo, yo, bo, co), (xp, yp, bp, cp))):
        scores = dot_nt(bm[...], cm[...])
        grad_scores = jnp.zeros((SPAN, SPAN), F32)
        for pair in range(HH // 2):
            cols = slice(pair * 128, (pair + 1) * 128)
            xs, ys = x[:, cols], y[:, cols]
            halves = []
            for side in range(2):
                h = b * HH + pair * 2 + side
                mine = jnp.where(low if side == 0 else ~low, xs, zero)
                grad_mixing = dot_nt(mine, ys)
                spread = small[2, h : h + 1, :] - cum_t[:, h : h + 1]
                decay = jnp.where(later, jnp.exp(jnp.minimum(spread, 0.0)), 0.0)
                mixing = scores * decay
                halves.append(dot(mixing.astype(BF), ys))
                scaled = grad_mixing * step_t[:, h : h + 1]
                grad_scores = grad_scores + scaled * decay
                sums_v[0, h : h + 1, :] = jnp.sum(scaled * mixing, axis=0, keepdims=True)
                col = jnp.sum(grad_mixing * mixing, axis=1, keepdims=True)
                sums = jnp.where(lane == h, col, sums)
            gs[b, :, cols] = jnp.where(low, halves[0], halves[1])
        gs_bf = grad_scores.astype(BF)
        gb[b] = dot(gs_bf, cm[...])
        gc[b] = dot(grad_scores.T.astype(BF), bm[...])
    sums_v[1] = sums.T[: 2 * HH]
    wait_all(copy_all([(sums_v, sums_out)], sems, 1))


def block_decays(small, decay):
    for b in range(2):
        last = jnp.exp(small[2, b * HH : (b + 1) * HH, SPAN - 1 :])
        spread = jnp.where(iota((HH, W), 1) // HD == iota((HH, W), 0), last, 0.0)
        decay[b] = jnp.broadcast_to(jnp.sum(spread, axis=0, keepdims=True), (8, W))


def assemble(scal, got, keep, decay, start, end, exact):
    first = scal[1]
    second = 1 - first
    for k in range(W // 128):
        cols = slice(k * 128, (k + 1) * 128)
        d_first, d_second = decay[first, 0:1, cols], decay[second, 0:1, cols]
        for r in range(N // PIECE):
            at = k * (N // PIECE) + r
            rows = slice(r * PIECE, (r + 1) * PIECE)
            s_in, e_in = got[at, 0:PIECE, :], got[at, PIECE : 2 * PIECE, :]
            start[first, rows, cols] = s_in
            end[second, rows, cols] = e_in
            s_f, e_f = s_in.astype(F32), e_in.astype(F32)
            s_next = d_first * s_f + keep[0, rows, cols].astype(F32)
            e_next = d_second * e_f + keep[1, rows, cols].astype(F32)
            start[second, rows, cols] = s_next.astype(BF)
            end[first, rows, cols] = e_next.astype(BF)
            if exact is not None:
                one = jnp.sum(s_f * e_next, axis=0, keepdims=True)
                two = jnp.sum(s_next * e_f, axis=0, keepdims=True)
                if r == 0:
                    sum_one, sum_two = one, two
                else:
                    sum_one, sum_two = sum_one + one, sum_two + two
        if exact is not None:
            exact[first, 0:1, cols] = sum_one
            exact[second, 0:1, cols] = sum_two


def head_map(shape, head_dim, chan_dim):
    return jnp.where(iota(shape, chan_dim) // HD == iota(shape, head_dim), 1.0, 0.0).astype(BF)


def pre_kernel(
    scal, got, keep_in, small_in, sums_in,
    xo, xp, yo, yp, bo, bp, co, cp, lo_in, lp_in,
    z0, z1, z2, z3, msg_out,
    start, end, exact, decay, keep, small, sums_v, rows_v, zed, msg, sems,
):
    early = copy_all([(small_in, small), (keep_in, keep)], sems)
    late = copy_all(
        [(sums_in, sums_v), (lo_in, rows_v.at[pl.ds(0, 128)]), (lp_in, rows_v.at[pl.ds(128, 128)])],
        sems,
        2,
    )
    wait_all(early)
    block_decays(small, decay)
    assemble(scal, got, keep, decay, start, end, exact)
    by_head = head_map((W, 128), 1, 0)
    sums = []
    joint = []
    for b, (x, y, bm, cm) in enumerate(((xo, yo, bo, co), (xp, yp, bp, cp))):
        for grad, mat, state in ((x, bm, end), (y, cm, start)):
            total = jnp.zeros((SPAN, 128), F32)
            for k in range(W // 256):
                cols = slice(k * 256, (k + 1) * 256)
                prod = dot(mat[...], state[b, :, cols]) * grad[:, cols].astype(F32)
                total = total + dot(prod.astype(BF), by_head[cols])
            sums.append(total.T[:HH])
        rows8 = jnp.concatenate(split3(exact[b, 0:1, :]) + [jnp.zeros((5, W), F32)], 0).astype(BF)
        joint.append(jnp.sum(dot_nt(head_map((HH, W), 0, 1), rows8), axis=1, keepdims=True))
    x_pulled = jnp.concatenate([sums[0], sums[2]], 0)
    y_state = jnp.concatenate([sums[1], sums[3]], 0)
    joint = jnp.concatenate(joint, 0)
    pre, step, cum = small[0], small[1], small[2]
    last = cum[:, SPAN - 1 :]
    rate = small[3]
    q = jnp.exp(last - cum) * x_pulled
    wait_all(late)
    cols = sums_v[1]
    u = sums_v[0] - step * cols + jnp.exp(cum) * y_state
    grad_log = (
        sum_by(u, triangle(lambda u, t: u >= t))
        + sum_by(step * q, triangle(lambda u, t: u < t))
        + jnp.exp(last) * joint
    )
    grad_step = cols + q - rate * grad_log
    grad_pre = grad_step * jax.nn.sigmoid(pre)
    rolled = pltpu.roll(grad_pre, scal[2], 1)
    for k in range(TP):
        turn = rolled if k == 0 else pltpu.roll(rolled, 128 - 32 * k, 1)
        zed[k] = turn.astype(BF)
    copies = copy_all([(zed.at[k], z) for k, z in enumerate((z0, z1, z2, z3))], sems, 5)
    rolled = jnp.concatenate([rolled[:HH], rolled[HH:]], 1).astype(BF)
    diagonal = iota((HH, 128), 0) == iota((HH, 128), 1)

    def as_row(v):
        v = v[:HH] + v[HH:]
        v = jnp.sum(v, axis=1, keepdims=True)
        return jnp.sum(jnp.where(diagonal, v, 0.0), axis=0, keepdims=True)

    extra = split3(as_row(grad_pre)) + split3(as_row(-grad_log * step))
    extra = jnp.concatenate(extra + [jnp.zeros((10, 128), F32)], 0).astype(BF)
    for k in range(D // 256):
        cols = slice(k * 256, (k + 1) * 256)
        part = dot(rolled, rows_v[:, cols])
        for j in range(2):
            msg[2 * k + j, 0:HH, :] = part[:, j * 128 : (j + 1) * 128].astype(BF)
            msg[2 * k + j, HH : 2 * HH, :] = extra
        if k % 4 == 3:
            done = pl.ds(2 * k - 6, 8)
            copies += copy_all([(msg.at[done], msg_out.at[done])], sems, 9 + k // 4)
    wait_all(copies)


def sum_kernel(msg, out, totals):
    total = jnp.zeros((2 * HH, 128), F32)
    for k in range(CHIPS):
        total = total + msg[k].astype(F32)
    rounded = total[:HH].astype(BF)
    for k in range(CHIPS):
        out[k] = rounded
    e = total[HH:]
    bias = e[0:1] + e[1:2] + e[2:3]
    rate = e[3:4] + e[4:5] + e[5:6]
    totals[...] = jnp.concatenate([bias, rate, jnp.zeros((6, 128), F32)], 0)


def grads_kernel(
    scal, got, keep_in, small_in, gs, gb, gc, maps,
    xo, xp, yo, yp, bo, bp, co, cp,
    gx_own, gx_other, bc_own, bc_other,
    start, end, decay, keep, small, sems,
):
    wait_all(copy_all([(small_in, small), (keep_in, keep)], sems))
    block_decays(small, decay)
    assemble(scal, got, keep, decay, start, end, None)
    step, cum = small[1], small[2]
    remain = jnp.exp(cum[:, SPAN - 1 :] - cum)
    growth = jnp.exp(cum)
    for b, (x, y, bm, cm) in enumerate(((xo, yo, bo, co), (xp, yp, bp, cp))):
        rows = slice(b * HH, (b + 1) * HH)
        w_a = columns(remain[rows], growth[rows])
        w_b = columns(step[rows], step[rows])
        grad_b, grad_c = gb[b], gc[b]
        gx_out, bc_out = ((gx_own, bc_own), (gx_other, bc_other))[b]
        for k in range(W // 256):
            cols = slice(k * 256, (k + 1) * 256)
            wide = slice(W + k * 256, W + (k + 1) * 256)
            remain_w = dot(w_a, maps[:, cols])
            step_w = dot(w_b, maps[:, cols])
            growth_w = dot(w_a, maps[:, wide])
            pulled = dot(bm[...], end[b, :, cols])
            gx_out[:, cols] = (step_w * (gs[b, :, cols] + remain_w * pulled)).astype(BF)
            in_w = (remain_w * (step_w * x[:, cols].astype(F32))).astype(BF)
            out_w = (growth_w * y[:, cols].astype(F32)).astype(BF)
            grad_b = grad_b + dot_nt(in_w, end[b, :, cols])
            grad_c = grad_c + dot_nt(out_w, start[b, :, cols])
        bc_out[0] = grad_b.astype(BF)
        bc_out[1] = grad_c.astype(BF)


def weight_kernel(scal, own, other, out):
    at_zero = scal[1] == 0
    for j in range(CHIPS):
        a, b = own[j].astype(F32), other[j].astype(F32)
        cols = slice(j * 128, (j + 1) * 128)
        out[0:HH, cols] = jnp.where(at_zero, a, b)
        out[HH : 2 * HH, cols] = jnp.where(at_zero, b, a)


def join_kernel(scal, gx_own, gx_other, bc_own, bc_other, gx, gb, gc):
    at_zero = scal[1] == 0

    def join(own, other, out, width):
        out[:, :width] = jnp.where(at_zero, own, other)
        out[:, width:] = jnp.where(at_zero, other, own)

    join(gx_own[...], gx_other[...], gx, W)
    join(bc_own[0], bc_other[0], gb, N)
    join(bc_own[1], bc_other[1], gc, N)


def input_kernel(scal, a0, a1, a2, a3, b0, b1, b2, b3, w0, w1, w2, w3, out):
    first = scal[1]
    mine = pl.ds(pl.multiple_of(HH * first, HH), HH)
    others = pl.ds(pl.multiple_of(HH * (1 - first), HH), HH)
    rows = []
    for a, b in ((a0, b0), (a1, b1), (a2, b2), (a3, b3)):
        rows += [a[:HH], b[HH:]]
    zed = jnp.concatenate(rows, 0).astype(F32).T[:32].astype(BF)
    for k in range(D // 512):
        cols = slice(k * 512, (k + 1) * 512)
        mats = []
        for w in (w0, w1, w2, w3):
            mats += [w[mine, cols], w[others, cols]]
        out[:, cols] = dot(zed, jnp.concatenate(mats, 0)).astype(BF)


def call(kernel, outs, args, scratch=(), sems=0, far_in=(), far_out=(), flops=0, moved=0, limit=16):
    near = pl.BlockSpec(memory_space=pltpu.VMEM)
    far = pl.BlockSpec(memory_space=pltpu.HBM)
    specs = []
    for i, a in enumerate(args):
        if a.dtype == jnp.int32:
            specs.append(pl.BlockSpec(memory_space=pltpu.SMEM))
        else:
            specs.append(far if i in far_in else near)
    shapes = [pltpu.VMEM(s, t) for s, t in scratch]
    if sems:
        shapes.append(pltpu.SemaphoreType.DMA((sems,)))
    return pl.pallas_call(
        kernel,
        out_shape=[jax.ShapeDtypeStruct(s, t) for s, t in outs],
        in_specs=specs,
        out_specs=[far if i in far_out else near for i in range(len(outs))],
        scratch_shapes=shapes,
        compiler_params=pltpu.CompilerParams(vmem_limit_bytes=limit * 2**20),
        cost_estimate=pl.CostEstimate(flops=flops, bytes_accessed=moved, transcendentals=0),
    )(*args)


def swap(v):
    return lax.ppermute(v, "core", [(0, 1), (1, 0)])


def round_tp(v, k):
    return lax.ppermute(v, "tp", [(i, (i + k) % TP) for i in range(TP)])


def local(layer_input, dt_weight, dt_bias, a_log, ssm_input, b_in, c_in, out_grad):
    core = lax.axis_index("core")
    tp = lax.axis_index("tp")
    scal = jnp.stack([32 * tp, core, (128 - 32 * tp) % 128]).astype(jnp.int32)

    def half(v, which, width, axis):
        return lax.dynamic_slice_in_dim(v, which * width, width, axis)

    pieces = [layer_input] + [
        lax.ppermute(layer_input, "tp", [((i + k) % TP, i) for i in range(TP)]) for k in (1, 3, 2)
    ]
    pieces = [pieces[0], pieces[1], pieces[3], pieces[2]]
    weight_t = dt_weight.T
    weight_mine = jnp.concatenate(
        [half(weight_t, core, HH, 0), half(weight_t, 1 - core, HH, 0)], 0
    )
    operands = []
    for v, width in ((ssm_input, W), (out_grad, W), (b_in, N), (c_in, N)):
        operands += [half(v, core, width, 1), swap(half(v, 1 - core, width, 1))]
    maps = spread_maps()
    small_t = ((4, 2 * HH, 128), F32)
    keep_t = ((2, N, W), BF)

    proj_own, proj_other, rows_own = call(
        project_kernel,
        [((HH, 128), F32)] * 2 + [((SPAN, D), BF)],
        [scal, weight_mine, dt_bias[None, :]] + pieces,
        sems=4,
        far_out=(2,),
        flops=2**26,
        moved=2**21,
    )
    proj_other = swap(proj_other)
    msg_t = ((CHIPS, 2 * PIECE + 8, 128), BF)
    msg, keep, small = call(
        state_kernel,
        [msg_t, keep_t, small_t],
        [scal, proj_own, proj_other, a_log[None, :]] + operands + [maps],
        [((2, N, W), F32), ((2, N, W), F32), ((2, 8, W), F32), msg_t, keep_t, small_t],
        sems=6,
        far_out=(0, 1, 2),
        flops=2**28,
        moved=2**22,
    )
    got = lax.all_to_all(msg, "chip", 0, 0, tiled=True)

    weight_t, rows_own = lax.optimization_barrier((weight_t, rows_own))
    weights = [weight_t] + [round_tp(weight_t, k) for k in (1, 2, 3)]
    rows_other = swap(rows_own)
    sums_t = ((2, 2 * HH, 128), F32)
    gs, gb, gc, sums = call(
        intra_kernel,
        [((2, SPAN, W), F32), ((2, SPAN, N), F32), ((2, SPAN, N), F32), sums_t],
        [small] + operands,
        [small_t, sums_t],
        sems=2,
        far_in=(0,),
        far_out=(3,),
    )

    (folded,) = call(
        fold_kernel, [((CHIPS, 2 * PIECE, 128), BF)], [got], flops=2**20, moved=2**20
    )
    states = lax.all_to_all(folded, "chip", 0, 0, tiled=True)

    states, weights = lax.optimization_barrier((states, weights))
    zed_t = ((2 * HH, 128), BF)
    parts_t = ((CHIPS, 2 * HH, 128), BF)
    state_scratch = [((2, N, W), BF), ((2, N, W), BF)]
    kept = [((2, 8, W), F32), keep_t, small_t]
    *zed, parts = call(
        pre_kernel,
        [zed_t] * 4 + [parts_t],
        [scal, states, keep, small, sums] + operands + [rows_own, rows_other],
        state_scratch
        + [((2, 8, W), F32)]
        + kept
        + [sums_t, ((2 * SPAN, D), BF), ((TP, 2 * HH, 128), BF), parts_t],
        sems=13,
        far_in=(2, 3, 4, 13, 14),
        far_out=(0, 1, 2, 3, 4),
        flops=2**29,
        moved=2**23,
    )
    shares = lax.all_to_all(parts, "chip", 0, 0, tiled=True)

    zed = [zed[0]] + [round_tp(zed[k], k) for k in (1, 2, 3)]
    (grad_layer_input,) = call(
        input_kernel, [((32, D), BF)], [scal] + zed + [swap(z) for z in zed] + weights
    )

    total, totals = call(
        sum_kernel, [((CHIPS, HH, 128), BF), ((8, 128), F32)], [shares], flops=2**20, moved=2**20
    )
    weight_own = lax.all_to_all(total, "chip", 0, 0, tiled=True)

    def join(mine, other, axis):
        return jnp.where(
            core == 0,
            jnp.concatenate([mine, other], axis),
            jnp.concatenate([other, mine], axis),
        )

    totals = join(totals[:2, :HH], swap(totals[:2, :HH]), 1)
    grad_dt_bias = totals[0]
    grad_a_log = jnp.exp(a_log) * totals[1]

    gs, total = lax.optimization_barrier((gs, total))
    gx_own, gx_other, bc_own, bc_other = call(
        grads_kernel,
        [((SPAN, W), BF)] * 2 + [((2, SPAN, N), BF)] * 2,
        [scal, states, keep, small, gs, gb, gc, maps] + operands,
        state_scratch + kept,
        sems=2,
        far_in=(2, 3),
    )
    grad_ssm_input, grad_b_in, grad_c_in = call(
        join_kernel,
        [((SPAN, 2 * W), BF), ((SPAN, 2 * N), BF), ((SPAN, 2 * N), BF)],
        [scal, gx_own, swap(gx_other), bc_own, swap(bc_other)],
    )

    (grad_dt_weight,) = call(
        weight_kernel,
        [((2 * HH, D), F32)],
        [scal, weight_own, swap(weight_own)],
        flops=2**20,
        moved=2**22,
    )
    return (
        grad_ssm_input,
        grad_b_in,
        grad_c_in,
        grad_layer_input,
        grad_dt_weight.T,
        grad_dt_bias,
        grad_a_log,
    )


def solution(mesh):
    fine = Mesh(mesh.devices.reshape(CHIPS, CORES, TP), ("chip", "core", "tp"))
    ctx = ("chip", "core")
    everything = ("chip", "core", "tp")
    placed = (
        P(everything, None),
        P(None, "tp"),
        P("tp"),
        P("tp"),
        P(ctx, "tp"),
        P(ctx, "tp"),
        P(ctx, "tp"),
        P(ctx, "tp"),
    )
    return jax.shard_map(
        local,
        mesh=fine,
        in_specs=placed,
        out_specs=(
            P(ctx, "tp"),
            P(ctx, "tp"),
            P(ctx, "tp"),
            P(everything, None),
            P(None, "tp"),
            P("tp"),
            P("tp"),
        ),
        check_vma=False,
    )
```

```python
import jax
import jax.numpy as jnp
from jax import lax
from jax.experimental import pallas as pl
from jax.experimental.pallas import tpu as pltpu
from jax.sharding import Mesh
from jax.sharding import PartitionSpec as P

LIMITS = 16, 16, 16, 16, 60
STATE_LIMIT, INTRA_LIMIT, PRE_LIMIT, GRADS_LIMIT, INPUT_LIMIT = LIMITS
BF = jnp.bfloat16
F32 = jnp.float32
CHIPS, CORES, TP = 32, 2, 4
SPAN = 128
N = 128
HD = 64
HH = 16
W = HH * HD
D = 4096
PIECE = 32


def dot(a, b):
    return lax.dot_general(a, b, (((1,), (0,)), ((), ())), preferred_element_type=F32)


def dot_nt(a, b):
    return lax.dot_general(a, b, (((1,), (1,)), ((), ())), preferred_element_type=F32)


def split3(v):
    hi = v.astype(BF).astype(F32)
    rest = v - hi
    mid = rest.astype(BF).astype(F32)
    return [hi, mid, rest - mid]


def iota(shape, dim):
    return lax.broadcasted_iota(jnp.int32, shape, dim)


def triangle(keep):
    return jnp.where(keep(iota((SPAN, SPAN), 0), iota((SPAN, SPAN), 1)), 1.0, 0.0).astype(BF)


def sum_by(rows, matrix):
    r = rows.shape[0]
    out = dot(jnp.concatenate(split3(rows), 0).astype(BF), matrix)
    return out[:r] + out[r : 2 * r] + out[2 * r :]


def columns(first, second):
    stack = split3(first) + split3(second) + [jnp.zeros((32, SPAN), F32)]
    return jnp.concatenate(stack, 0).T.astype(BF)


def spreader():
    row = iota((128, 256), 0)
    off = row % HH - iota((128, 256), 1) // HD
    offs = [jnp.where(row // 48 == part, off, -99) for part in range(2)]

    def spread(cols, part, k):
        return dot(cols, jnp.where(offs[part] == 4 * k, 1.0, 0.0).astype(BF))

    return spread


def copy_all(pairs, sems, first=0):
    copies = [pltpu.make_async_copy(a, b, sems.at[first + i]) for i, (a, b) in enumerate(pairs)]
    for c in copies:
        c.start()
    return copies


def wait_all(copies):
    for c in copies:
        c.wait()


def parts_of(pack):
    views = []
    for at, width in ((0, W), (W, W), (2 * W, N), (2 * W + N, N)):
        views.append(pack.at[:, pl.ds(at, width)])
    return views


def pack_kernel(scal, x, y, bm, cm, mine, theirs):
    first = scal[1]
    for out, side in ((mine, first), (theirs, 1 - first)):
        at = 0
        for v, width in ((x, W), (y, W), (bm, N), (cm, N)):
            place = pl.ds(pl.multiple_of(side * width, width), width)
            out[:, at : at + width] = v[:, place]
            at += width


def project_kernel(scal, w, params, l0, l1, l2, l3, own, other):
    first = scal[1]
    head = iota((2 * HH, 2 * HH), 0)
    head = jnp.where(first == 0, head, lax.rem(head + HH, 2 * HH))
    mine = iota((2 * HH, 2 * HH), 1) == head
    add = jnp.sum(jnp.where(mine, params[0:1], 0.0), axis=1, keepdims=True)
    rate = jnp.exp(jnp.sum(jnp.where(mine, params[1:2], 0.0), axis=1, keepdims=True))
    own[1] = jnp.broadcast_to(rate[:HH], (HH, 128))
    rows = jnp.concatenate([l0[...], l1[...], l2[...], l3[...]], 0)
    acc = pltpu.roll(dot_nt(w[...], rows), scal[0], 1) + add
    own[0] = acc[:HH]
    other[...] = acc[HH:]


def state_kernel(
    scal, po, pp, own, other,
    msg_out, keep, small,
    s_all, p_all, decay, msg, sems,
):
    first = scal[1]
    second = 1 - first
    pre = jnp.concatenate([po[0], pp[...]], 0)
    step = jnp.maximum(pre, 0.0) + jnp.log1p(jnp.exp(-jnp.abs(pre)))
    rate = jnp.concatenate([po[1], po[1]], 0)
    cum = sum_by(-rate * step, triangle(lambda u, t: u <= t))
    small[0] = pre
    small[1] = step
    small[2] = cum
    small[3] = rate
    copies = []
    spread = spreader()
    remain_step = jnp.exp(cum[:, SPAN - 1 :] - cum) * step
    growth = jnp.exp(cum)
    for b, (x, y, bm, cm) in enumerate((parts_of(own), parts_of(other))):
        rows = slice(b * HH, (b + 1) * HH)
        weights = columns(remain_step[rows], growth[rows])
        b_t = bm[...].astype(F32).T.astype(BF)
        c_t = cm[...].astype(F32).T.astype(BF)
        for k in range(W // 256):
            cols = slice(k * 256, (k + 1) * 256)
            w_in = spread(weights, 0, k)
            s_all[b, :, cols] = dot(b_t, (w_in * x[:, cols].astype(F32)).astype(BF))
            w_out = spread(weights, 1, k)
            p_all[b, :, cols] = dot(c_t, (w_out * y[:, cols].astype(F32)).astype(BF))
            decay[b, :, cols] = jnp.broadcast_to(w_out[SPAN - 1 :], (8, 256))
    per = N // PIECE
    for k in range(W // 128):
        cols = slice(k * 128, (k + 1) * 128)
        d_first, d_second = decay[first, 0:1, cols], decay[second, 0:1, cols]
        s_f, p_s = s_all[first, :, cols], p_all[second, :, cols]
        forward = d_second * s_f + s_all[second, :, cols]
        backward = p_all[first, :, cols] + d_first * p_s
        keep[0, :, cols] = s_f.astype(BF)
        keep[1, :, cols] = p_s.astype(BF)
        d3 = split3(d_first * d_second) + [jnp.zeros((5, 128), F32)]
        for r in range(per):
            rows = slice(r * PIECE, (r + 1) * PIECE)
            whole = jnp.concatenate([forward[rows], backward[rows]] + d3, 0)
            msg[k * per + r] = whole.astype(BF)
        if k % 2 == 1:
            done = pl.ds((k - 1) * per, 2 * per)
            copies += copy_all([(msg.at[done], msg_out.at[done])], sems, k // 2)
    wait_all(copies)


def fold_kernel(msg, out):
    parts = [msg[k].astype(F32) for k in range(CHIPS)]
    decays = [v[2 * PIECE : 2 * PIECE + 1] + v[2 * PIECE + 1 : 2 * PIECE + 2] + v[2 * PIECE + 2 : 2 * PIECE + 3] for v in parts]
    total = jnp.zeros((PIECE, 128), F32)
    for k in range(CHIPS):
        out[k, 0:PIECE, :] = total.astype(BF)
        total = total * decays[k] + parts[k][:PIECE]
    total = jnp.zeros((PIECE, 128), F32)
    for k in reversed(range(CHIPS)):
        out[k, PIECE : 2 * PIECE, :] = total.astype(BF)
        total = total * decays[k] + parts[k][PIECE : 2 * PIECE]


def intra_kernel(
    small, own, other,
    wide, gb, gc, sums_v,
    gs,
):
    spread = spreader()
    step, cum = small[1], small[2]
    remain = jnp.exp(cum[:, SPAN - 1 :] - cum)
    growth = jnp.exp(cum)
    lane = iota((SPAN, 128), 1)
    low = lane < HD
    later = lane >= iota((SPAN, SPAN), 0)
    step_t = jnp.concatenate([small[1], jnp.zeros((96, 128), F32)], 0).T
    cum_t = jnp.concatenate([small[2], jnp.zeros((96, 128), F32)], 0).T
    sums = jnp.zeros((SPAN, 128), F32)
    zero = jnp.zeros((SPAN, 128), BF)
    for b, (x, y, bm, cm) in enumerate((parts_of(own), parts_of(other))):
        scores = dot_nt(bm[...], cm[...])
        grad_scores = jnp.zeros((SPAN, SPAN), F32)
        for pair in range(HH // 2):
            cols = slice(pair * 128, (pair + 1) * 128)
            xs, ys = x[:, cols], y[:, cols]
            halves = []
            for side in range(2):
                h = b * HH + pair * 2 + side
                mine = jnp.where(low if side == 0 else ~low, xs, zero)
                grad_mixing = dot_nt(mine, ys)
                gap = small[2, h : h + 1, :] - cum_t[:, h : h + 1]
                decay = jnp.where(later, jnp.exp(jnp.minimum(gap, 0.0)), 0.0)
                mixing = scores * decay
                halves.append(dot(mixing.astype(BF), ys))
                scaled = grad_mixing * step_t[:, h : h + 1]
                grad_scores = grad_scores + scaled * decay
                sums_v[0, h : h + 1, :] = jnp.sum(scaled * mixing, axis=0, keepdims=True)
                col = jnp.sum(grad_mixing * mixing, axis=1, keepdims=True)
                sums = jnp.where(lane == h, col, sums)
            gs[b, :, cols] = jnp.where(low, halves[0], halves[1])
        rows = slice(b * HH, (b + 1) * HH)
        w_a = columns(remain[rows] * step[rows], growth[rows])
        w_b = columns(step[rows], step[rows])
        for k in range(W // 256):
            cols = slice(k * 256, (k + 1) * 256)
            remain_w = spread(w_a, 0, k)
            wide[1, b, :, cols] = remain_w.astype(BF)
            wide[2, b, :, cols] = (remain_w * x[:, cols].astype(F32)).astype(BF)
            wide[3, b, :, cols] = (spread(w_a, 1, k) * y[:, cols].astype(F32)).astype(BF)
            wide[0, b, :, cols] = (gs[b, :, cols] * spread(w_b, 0, k)).astype(BF)
        gs_bf = grad_scores.astype(BF)
        gb[b] = dot(gs_bf, cm[...])
        gc[b] = dot(grad_scores.T.astype(BF), bm[...])
    sums_v[1] = sums.T[: 2 * HH]


def block_decays(small, decay):
    for b in range(2):
        last = jnp.exp(small[2, b * HH : (b + 1) * HH, SPAN - 1 :])
        spread = jnp.where(iota((HH, W), 1) // HD == iota((HH, W), 0), last, 0.0)
        decay[b] = jnp.broadcast_to(jnp.sum(spread, axis=0, keepdims=True), (8, W))


def assemble(scal, got, keep, decay, start, end, exact):
    first = scal[1]
    second = 1 - first
    for k in range(W // 128):
        cols = slice(k * 128, (k + 1) * 128)
        d_first, d_second = decay[first, 0:1, cols], decay[second, 0:1, cols]
        for r in range(N // PIECE):
            at = k * (N // PIECE) + r
            rows = slice(r * PIECE, (r + 1) * PIECE)
            s_in, e_in = got[at, 0:PIECE, :], got[at, PIECE : 2 * PIECE, :]
            start[first, rows, cols] = s_in
            end[second, rows, cols] = e_in
            s_f, e_f = s_in.astype(F32), e_in.astype(F32)
            s_next = d_first * s_f + keep[0, rows, cols].astype(F32)
            e_next = d_second * e_f + keep[1, rows, cols].astype(F32)
            start[second, rows, cols] = s_next.astype(BF)
            end[first, rows, cols] = e_next.astype(BF)
            if exact is not None:
                one = jnp.sum(s_f * e_next, axis=0, keepdims=True)
                two = jnp.sum(s_next * e_f, axis=0, keepdims=True)
                if r == 0:
                    sum_one, sum_two = one, two
                else:
                    sum_one, sum_two = sum_one + one, sum_two + two
        if exact is not None:
            exact[first, 0:1, cols] = sum_one
            exact[second, 0:1, cols] = sum_two


def head_map(shape, head_dim, chan_dim):
    return jnp.where(iota(shape, chan_dim) // HD == iota(shape, head_dim), 1.0, 0.0).astype(BF)


def pre_kernel(
    scal, got, keep, small, sums_v, own, other, lo_in, lp_in,
    zed_own, zed_other, msg_out,
    start, end, exact, decay, rows_v, msg, sems,
):
    late = copy_all(
        [(v, rows_v.at[pl.ds(SPAN * k, SPAN)]) for k, v in enumerate((lo_in, lp_in))], sems, 4
    )
    block_decays(small, decay)
    assemble(scal, got, keep, decay, start, end, exact)
    by_head = head_map((W, 128), 1, 0)
    sums = []
    joint = []
    for b, (x, y, bm, cm) in enumerate((parts_of(own), parts_of(other))):
        for grad, mat, state in ((x, bm, end), (y, cm, start)):
            total = jnp.zeros((SPAN, 128), F32)
            for k in range(W // 256):
                cols = slice(k * 256, (k + 1) * 256)
                prod = dot(mat[...], state[b, :, cols]) * grad[:, cols].astype(F32)
                total = total + dot(prod.astype(BF), by_head[cols])
            sums.append(total.T[:HH])
        rows8 = jnp.concatenate(split3(exact[b, 0:1, :]) + [jnp.zeros((5, W), F32)], 0).astype(BF)
        joint.append(jnp.sum(dot_nt(head_map((HH, W), 0, 1), rows8), axis=1, keepdims=True))
    x_pulled = jnp.concatenate([sums[0], sums[2]], 0)
    y_state = jnp.concatenate([sums[1], sums[3]], 0)
    joint = jnp.concatenate(joint, 0)
    pre, step, cum = small[0], small[1], small[2]
    last = cum[:, SPAN - 1 :]
    rate = small[3]
    q = jnp.exp(last - cum) * x_pulled
    cols = sums_v[1]
    u = sums_v[0] - step * cols + jnp.exp(cum) * y_state
    grad_log = (
        sum_by(u, triangle(lambda u, t: u >= t))
        + sum_by(step * q, triangle(lambda u, t: u < t))
        + jnp.exp(last) * joint
    )
    grad_step = cols + q - rate * grad_log
    grad_pre = grad_step * jax.nn.sigmoid(pre)
    rolled = pltpu.roll(grad_pre, scal[2], 1)
    for k in range(TP):
        turn = rolled if k == 0 else pltpu.roll(rolled, 128 - 32 * k, 1)
        zed_own[k] = turn[:HH].astype(BF)
        zed_other[k] = turn[HH:].astype(BF)
    copies = []
    rolled = jnp.concatenate([rolled[:HH], rolled[HH:]], 1).astype(BF)
    diagonal = iota((HH, 128), 0) == iota((HH, 128), 1)

    def as_row(v):
        v = v[:HH] + v[HH:]
        v = jnp.sum(v, axis=1, keepdims=True)
        return jnp.sum(jnp.where(diagonal, v, 0.0), axis=0, keepdims=True)

    wait_all(late)
    extra = split3(as_row(grad_pre)) + split3(as_row(-grad_log * step))
    extra = jnp.concatenate(extra + [jnp.zeros((10, 128), F32)], 0).astype(BF)
    for k in range(D // 256):
        cols = slice(k * 256, (k + 1) * 256)
        part = dot(rolled, rows_v[:, cols])
        for j in range(2):
            msg[2 * k + j, 0:HH, :] = part[:, j * 128 : (j + 1) * 128].astype(BF)
            msg[2 * k + j, HH : 2 * HH, :] = extra
        if k % 4 == 3:
            done = pl.ds(2 * k - 6, 8)
            copies += copy_all([(msg.at[done], msg_out.at[done])], sems, k // 4)
    wait_all(copies)


def sum_kernel(msg, out, totals):
    total = jnp.zeros((2 * HH, 128), F32)
    for k in range(CHIPS):
        total = total + msg[k].astype(F32)
    rounded = total[:HH].astype(BF)
    for k in range(CHIPS):
        out[k] = rounded
    e = total[HH:]
    bias = e[0:1] + e[1:2] + e[2:3]
    rate = e[3:4] + e[4:5] + e[5:6]
    totals[...] = jnp.concatenate([bias, rate, jnp.zeros((6, 128), F32)], 0)


def grads_kernel(
    scal, got, keep, small, wide_in, gb, gc, own, other, totals,
    out_own, out_other,
    start, end, decay, wide, sems,
):
    loads = copy_all([(wide_in, wide)], sems)
    gs, remain, in_w, out_w = [wide.at[i] for i in range(4)]
    block_decays(small, decay)
    assemble(scal, got, keep, decay, start, end, None)
    wait_all(loads)
    for b, bm in enumerate((parts_of(own)[2], parts_of(other)[2])):
        grad_b, grad_c = gb[b], gc[b]
        out = (out_own, out_other)[b]
        for k in range(W // 256):
            cols = slice(k * 256, (k + 1) * 256)
            pulled = dot(bm[...], end[b, :, cols])
            out[:SPAN, cols] = (
                gs[b, :, cols].astype(F32) + remain[b, :, cols].astype(F32) * pulled
            ).astype(BF)
            grad_b = grad_b + dot_nt(in_w[b, :, cols], end[b, :, cols])
            grad_c = grad_c + dot_nt(out_w[b, :, cols], start[b, :, cols])
        out[:SPAN, W : W + N] = grad_b.astype(BF)
        out[:SPAN, W + N :] = grad_c.astype(BF)
        spare = jnp.concatenate(split3(totals[...]) + [jnp.zeros((8, 128), F32)], 0)
        out[SPAN:, :128] = spare.astype(BF)


def weight_kernel(scal, own, other, out):
    at_zero = scal[1] == 0
    for j in range(CHIPS):
        a, b = own[j].astype(F32), other[j].astype(F32)
        cols = slice(j * 128, (j + 1) * 128)
        out[0:HH, cols] = jnp.where(at_zero, a, b)
        out[HH : 2 * HH, cols] = jnp.where(at_zero, b, a)


def join_kernel(scal, own, other, params, gx, gb, gc, g_bias, g_rate):
    at_zero = scal[1] == 0

    def join(a, b):
        return jnp.where(at_zero, a, b), jnp.where(at_zero, b, a)

    for out, at, width in ((gx, 0, W), (gb, W, N), (gc, W + N, N)):
        cols = slice(at, at + width)
        out[:, :width], out[:, width:] = join(own[:SPAN, cols], other[:SPAN, cols])
    sums = []
    for v in (own, other):
        v = v[SPAN:, :128].astype(F32)
        sums.append(v[:8] + v[8:16] + v[16:24])
    low, high = join(*sums)
    lane = iota((8, 128), 1)
    total = jnp.where(lane < HH, low, pltpu.roll(high, HH, 1))
    g_bias[...] = total[0:1, : 2 * HH]
    g_rate[...] = total[1:2, : 2 * HH] * jnp.exp(params[1:2])


def turn_kernel(own, other, *outs):
    for k, out in enumerate(outs):
        out[:HH] = own[k]
        out[HH:] = other[k]


def input_kernel(scal, a0, a1, a2, a3, w0, w1, w2, w3, out, mat, sems):
    first = scal[1]
    copies = []
    for k, w in enumerate((w0, w1, w2, w3)):
        for j, side in enumerate((first, 1 - first)):
            part = w.at[pl.ds(pl.multiple_of(HH * side, HH), HH)]
            place = mat.at[pl.ds(2 * HH * k + HH * j, HH)]
            copies += copy_all([(part, place)], sems, 2 * k + j)
    rows = [a[...] for a in (a0, a1, a2, a3)]
    zed = jnp.concatenate(rows, 0).astype(F32).T[:32].astype(BF)
    wait_all(copies)
    for k in range(D // 512):
        cols = slice(k * 512, (k + 1) * 512)
        out[:, cols] = dot(zed, mat[:, cols]).astype(BF)


def call(kernel, outs, args, scratch=(), sems=0, far_in=(), far_out=(), flops=0, moved=0, limit=16):
    near = pl.BlockSpec(memory_space=pltpu.VMEM)
    far = pl.BlockSpec(memory_space=pltpu.HBM)
    specs = []
    for i, a in enumerate(args):
        if a.dtype == jnp.int32:
            specs.append(pl.BlockSpec(memory_space=pltpu.SMEM))
        else:
            specs.append(far if i in far_in else near)
    shapes = [pltpu.VMEM(s, t) for s, t in scratch]
    if sems:
        shapes.append(pltpu.SemaphoreType.DMA((sems,)))
    return pl.pallas_call(
        kernel,
        out_shape=[jax.ShapeDtypeStruct(s, t) for s, t in outs],
        in_specs=specs,
        out_specs=[far if i in far_out else near for i in range(len(outs))],
        scratch_shapes=shapes,
        compiler_params=pltpu.CompilerParams(vmem_limit_bytes=int(limit * 2**20)),
        cost_estimate=pl.CostEstimate(flops=flops, bytes_accessed=moved, transcendentals=0),
    )(*args)


def swap(v):
    return lax.ppermute(v, "core", [(0, 1), (1, 0)])


def round_tp(v, k):
    return lax.ppermute(v, "tp", [(i, (i + k) % TP) for i in range(TP)])


def local(layer_input, dt_weight, dt_bias, a_log, ssm_input, b_in, c_in, out_grad):
    core = lax.axis_index("core")
    tp = lax.axis_index("tp")
    scal = jnp.stack([32 * tp, core, (128 - 32 * tp) % 128]).astype(jnp.int32)

    def half(v, which, width, axis):
        return lax.dynamic_slice_in_dim(v, which * width, width, axis)

    pieces = [layer_input] + [
        lax.ppermute(layer_input, "tp", [((i + k) % TP, i) for i in range(TP)]) for k in (1, 3, 2)
    ]
    pieces = [pieces[0], pieces[1], pieces[3], pieces[2]]
    weight_t = dt_weight.T
    weight_mine = jnp.concatenate(
        [half(weight_t, core, HH, 0), half(weight_t, 1 - core, HH, 0)], 0
    )
    pack_t = ((SPAN, 2 * W + 2 * N), BF)
    mine, theirs = call(pack_kernel, [pack_t] * 2, [scal, ssm_input, out_grad, b_in, c_in])
    operands = [mine, swap(theirs)]
    params = jnp.stack([dt_bias, a_log])
    small_t = ((4, 2 * HH, 128), F32)
    keep_t = ((2, N, W), BF)

    proj_own, proj_other = call(
        project_kernel,
        [((2, HH, 128), F32), ((HH, 128), F32)],
        [scal, weight_mine, params] + pieces,
        limit=16,
        flops=2**26,
        moved=2**21,
    )
    proj_other = swap(proj_other)
    msg_t = ((CHIPS, 2 * PIECE + 8, 128), BF)
    msg, keep, small = call(
        state_kernel,
        [msg_t, keep_t, small_t],
        [scal, proj_own, proj_other] + operands,
        [((2, N, W), F32), ((2, N, W), F32), ((2, 8, W), F32), msg_t],
        sems=4,
        far_out=(0,),
        limit=STATE_LIMIT,
        flops=2**28,
        moved=2**22,
    )
    got = lax.all_to_all(msg, "chip", 0, 0, tiled=True)

    weight_t, small = lax.optimization_barrier((weight_t, small))
    near = [round_tp(weight_t, k) for k in (1, 3)]
    far = round_tp(weight_t, 2)
    rows_own = jnp.concatenate(pieces, 0)
    rows_other = swap(rows_own)
    sums_t = ((2, 2 * HH, 128), F32)
    wide_t = ((4, 2, SPAN, W), BF)
    wide, gb, gc, sums = call(
        intra_kernel,
        [wide_t, ((2, SPAN, N), F32), ((2, SPAN, N), F32), sums_t],
        [small] + operands,
        [((2, SPAN, W), F32)],
        limit=INTRA_LIMIT,
    )

    got, near = lax.optimization_barrier((got, near))
    (folded,) = call(
        fold_kernel, [((CHIPS, 2 * PIECE, 128), BF)], [got], flops=2**20, moved=2**20, limit=16
    )
    states = lax.all_to_all(folded, "chip", 0, 0, tiled=True)
    states, far = lax.optimization_barrier((states, far))
    weights = [weight_t, near[0], far, near[1]]

    parts_t = ((CHIPS, 2 * HH, 128), BF)
    state_scratch = [((2, N, W), BF), ((2, N, W), BF)]
    zed_own, zed_other, parts = call(
        pre_kernel,
        [((TP, HH, 128), BF)] * 2 + [parts_t],
        [scal, states, keep, small, sums] + operands + [rows_own, rows_other],
        state_scratch
        + [((2, 8, W), F32), ((2, 8, W), F32), ((2 * SPAN, D), BF), parts_t],
        sems=6,
        far_in=(7, 8),
        far_out=(2,),
        flops=2**29,
        moved=2**23,
        limit=PRE_LIMIT,
    )
    shares = lax.all_to_all(parts, "chip", 0, 0, tiled=True)

    zed = call(turn_kernel, [((2 * HH, 128), BF)] * TP, [zed_own, swap(zed_other)])
    zed = [zed[0]] + [round_tp(zed[k], k) for k in (1, 2, 3)]
    shares, zed = lax.optimization_barrier((shares, zed))
    total, totals = call(
        sum_kernel, [((CHIPS, HH, 128), BF), ((8, 128), F32)], [shares], flops=2**20, moved=2**20, limit=16
    )
    weight_own = lax.all_to_all(total, "chip", 0, 0, tiled=True)

    wide, zed, total = lax.optimization_barrier((wide, zed, total))
    (grad_layer_input,) = call(
        input_kernel,
        [((32, D), BF)],
        [scal] + zed + weights,
        [((TP * 2 * HH, D), BF)],
        sems=8,
        far_in=(5, 6, 7, 8),
        limit=INPUT_LIMIT,
    )

    out_t = ((SPAN + 32, W + 2 * N), BF)
    out_own, out_other = call(
        grads_kernel,
        [out_t] * 2,
        [scal, states, keep, small, wide, gb, gc] + operands + [totals],
        state_scratch + [((2, 8, W), F32), wide_t],
        sems=1,
        far_in=(4,),
        limit=GRADS_LIMIT,
    )
    weight_own, out_own, out_other, grad_layer_input = lax.optimization_barrier(
        (weight_own, out_own, out_other, grad_layer_input)
    )
    joined = call(
        join_kernel,
        [((SPAN, 2 * W), BF), ((SPAN, 2 * N), BF), ((SPAN, 2 * N), BF)] + [((1, 2 * HH), F32)] * 2,
        [scal, out_own, swap(out_other), params],
    )
    grad_ssm_input, grad_b_in, grad_c_in, grad_dt_bias, grad_a_log = joined

    (grad_dt_weight,) = call(
        weight_kernel,
        [((2 * HH, D), F32)],
        [scal, weight_own, swap(weight_own)],
        flops=2**20,
        moved=2**22,
    )
    return (
        grad_ssm_input,
        grad_b_in,
        grad_c_in,
        grad_layer_input,
        grad_dt_weight.T,
        grad_dt_bias[0],
        grad_a_log[0],
    )


def solution(mesh):
    fine = Mesh(mesh.devices.reshape(CHIPS, CORES, TP), ("chip", "core", "tp"))
    ctx = ("chip", "core")
    everything = ("chip", "core", "tp")
    placed = (
        P(everything, None),
        P(None, "tp"),
        P("tp"),
        P("tp"),
        P(ctx, "tp"),
        P(ctx, "tp"),
        P(ctx, "tp"),
        P(ctx, "tp"),
    )
    return jax.shard_map(
        local,
        mesh=fine,
        in_specs=placed,
        out_specs=(
            P(ctx, "tp"),
            P(ctx, "tp"),
            P(ctx, "tp"),
            P(everything, None),
            P(None, "tp"),
            P("tp"),
            P("tp"),
        ),
        check_vma=False,
    )
```

```python
import jax
import jax.numpy as jnp
from jax import lax
from jax.experimental import pallas as pl
from jax.experimental.pallas import tpu as pltpu
from jax.sharding import Mesh
from jax.sharding import PartitionSpec as P

LIMITS = 16, 16, 16, 16, 60
STATE_LIMIT, INTRA_LIMIT, PRE_LIMIT, GRADS_LIMIT, INPUT_LIMIT = LIMITS
BF = jnp.bfloat16
F32 = jnp.float32
CHIPS, CORES, TP = 32, 2, 4
SPAN = 128
N = 128
HD = 64
HH = 16
W = HH * HD
D = 4096
PIECE = 32


def dot(a, b):
    return lax.dot_general(a, b, (((1,), (0,)), ((), ())), preferred_element_type=F32)


def dot_nt(a, b):
    return lax.dot_general(a, b, (((1,), (1,)), ((), ())), preferred_element_type=F32)


def split3(v):
    hi = v.astype(BF).astype(F32)
    rest = v - hi
    mid = rest.astype(BF).astype(F32)
    return [hi, mid, rest - mid]


def iota(shape, dim):
    return lax.broadcasted_iota(jnp.int32, shape, dim)


def triangle(keep):
    return jnp.where(keep(iota((SPAN, SPAN), 0), iota((SPAN, SPAN), 1)), 1.0, 0.0).astype(BF)


def sum_by(rows, matrix):
    r = rows.shape[0]
    out = dot(jnp.concatenate(split3(rows), 0).astype(BF), matrix)
    return out[:r] + out[r : 2 * r] + out[2 * r :]


def columns(first, second):
    stack = split3(first) + split3(second) + [jnp.zeros((32, SPAN), F32)]
    return jnp.concatenate(stack, 0).T.astype(BF)


def spreader():
    row = iota((128, 256), 0)
    off = row % HH - iota((128, 256), 1) // HD
    offs = [jnp.where(row // 48 == part, off, -99) for part in range(2)]

    def spread(cols, part, k):
        return dot(cols, jnp.where(offs[part] == 4 * k, 1.0, 0.0).astype(BF))

    return spread


def copy_all(pairs, sems, first=0):
    copies = [pltpu.make_async_copy(a, b, sems.at[first + i]) for i, (a, b) in enumerate(pairs)]
    for c in copies:
        c.start()
    return copies


def wait_all(copies):
    for c in copies:
        c.wait()


def parts_of(pack):
    views = []
    for at, width in ((0, W), (W, W), (2 * W, N), (2 * W + N, N)):
        views.append(pack.at[:, pl.ds(at, width)])
    return views


def pack_kernel(scal, x, y, bm, cm, mine, theirs):
    first = scal[1]
    for out, side in ((mine, first), (theirs, 1 - first)):
        at = 0
        for v, width in ((x, W), (y, W), (bm, N), (cm, N)):
            place = pl.ds(pl.multiple_of(side * width, width), width)
            out[:, at : at + width] = v[:, place]
            at += width


def project_kernel(scal, w, params, l3, l2, l1, l0, own, other):
    first = scal[1]
    head = iota((2 * HH, 2 * HH), 0)
    head = jnp.where(first == 0, head, lax.rem(head + HH, 2 * HH))
    mine = iota((2 * HH, 2 * HH), 1) == head
    add = jnp.sum(jnp.where(mine, params[0:1], 0.0), axis=1, keepdims=True)
    rate = jnp.exp(jnp.sum(jnp.where(mine, params[1:2], 0.0), axis=1, keepdims=True))
    own[1] = jnp.broadcast_to(rate[:HH], (HH, 128))
    rows = jnp.concatenate([l0[...], l1[...], l2[...], l3[...]], 0)
    acc = pltpu.roll(dot_nt(w[...], rows), scal[0], 1) + add
    own[0] = acc[:HH]
    other[...] = acc[HH:]


def state_kernel(
    scal, po, pp, own, other,
    msg, keep, small,
    s_all, p_all, decay,
):
    first = scal[1]
    second = 1 - first
    pre = jnp.concatenate([po[0], pp[...]], 0)
    step = jnp.maximum(pre, 0.0) + jnp.log1p(jnp.exp(-jnp.abs(pre)))
    rate = jnp.concatenate([po[1], po[1]], 0)
    cum = sum_by(-rate * step, triangle(lambda u, t: u <= t))
    small[0] = pre
    small[1] = step
    small[2] = cum
    small[3] = rate
    spread = spreader()
    remain_step = jnp.exp(cum[:, SPAN - 1 :] - cum) * step
    growth = jnp.exp(cum)
    weights = [columns(remain_step[i : i + HH], growth[i : i + HH]) for i in (0, HH)]
    weights = jnp.concatenate(weights, 0)
    blocks = (parts_of(own), parts_of(other))
    mats = [[v[...].astype(F32).T.astype(BF) for v in block[2:]] for block in blocks]
    for k in range(W // 256):
        cols = slice(k * 256, (k + 1) * 256)
        w_in, w_out = spread(weights, 0, k), spread(weights, 1, k)
        for b, (x, y, _, _) in enumerate(blocks):
            rows = slice(b * SPAN, (b + 1) * SPAN)
            x_w = (w_in[rows] * x[:, cols].astype(F32)).astype(BF)
            y_w = (w_out[rows] * y[:, cols].astype(F32)).astype(BF)
            s_all[b, :, cols] = dot(mats[b][0], x_w)
            p_all[b, :, cols] = dot(mats[b][1], y_w)
            last = (b + 1) * SPAN - 1
            decay[b, :, cols] = jnp.broadcast_to(w_out[last : last + 1], (8, 256))
    per = N // PIECE
    for k in range(W // 128):
        cols = slice(k * 128, (k + 1) * 128)
        d_first, d_second = decay[first, 0:1, cols], decay[second, 0:1, cols]
        s_f, p_s = s_all[first, :, cols], p_all[second, :, cols]
        forward = d_second * s_f + s_all[second, :, cols]
        backward = p_all[first, :, cols] + d_first * p_s
        keep[0, :, cols] = s_f.astype(BF)
        keep[1, :, cols] = p_s.astype(BF)
        d3 = split3(d_first * d_second) + [jnp.zeros((5, 128), F32)]
        for r in range(per):
            rows = slice(r * PIECE, (r + 1) * PIECE)
            whole = jnp.concatenate([forward[rows], backward[rows]] + d3, 0)
            msg[k * per + r] = whole.astype(BF)


def fold_kernel(msg, out):
    parts = [msg[k].astype(F32) for k in range(CHIPS)]
    decays = [v[2 * PIECE : 2 * PIECE + 1] + v[2 * PIECE + 1 : 2 * PIECE + 2] + v[2 * PIECE + 2 : 2 * PIECE + 3] for v in parts]
    total = jnp.zeros((PIECE, 128), F32)
    for k in range(CHIPS):
        out[k, 0:PIECE, :] = total.astype(BF)
        total = total * decays[k] + parts[k][:PIECE]
    total = jnp.zeros((PIECE, 128), F32)
    for k in reversed(range(CHIPS)):
        out[k, PIECE : 2 * PIECE, :] = total.astype(BF)
        total = total * decays[k] + parts[k][PIECE : 2 * PIECE]


def intra_kernel(
    small, own, other,
    wide, gb, gc, sums_v,
    gs,
):
    spread = spreader()
    step, cum = small[1], small[2]
    remain = jnp.exp(cum[:, SPAN - 1 :] - cum)
    growth = jnp.exp(cum)
    lane = iota((SPAN, 128), 1)
    low = lane < HD
    later = lane >= iota((SPAN, SPAN), 0)
    step_t = jnp.concatenate([small[1], jnp.zeros((96, 128), F32)], 0).T
    cum_t = jnp.concatenate([small[2], jnp.zeros((96, 128), F32)], 0).T
    sums = jnp.zeros((SPAN, 128), F32)
    zero = jnp.zeros((SPAN, 128), BF)
    for b, (x, y, bm, cm) in enumerate((parts_of(own), parts_of(other))):
        scores = dot_nt(bm[...], cm[...])
        grad_scores = jnp.zeros((SPAN, SPAN), F32)
        for pair in range(HH // 2):
            cols = slice(pair * 128, (pair + 1) * 128)
            xs, ys = x[:, cols], y[:, cols]
            halves = []
            for side in range(2):
                h = b * HH + pair * 2 + side
                mine = jnp.where(low if side == 0 else ~low, xs, zero)
                grad_mixing = dot_nt(mine, ys)
                gap = small[2, h : h + 1, :] - cum_t[:, h : h + 1]
                decay = jnp.where(later, jnp.exp(jnp.minimum(gap, 0.0)), 0.0)
                mixing = scores * decay
                halves.append(dot(mixing.astype(BF), ys))
                scaled = grad_mixing * step_t[:, h : h + 1]
                grad_scores = grad_scores + scaled * decay
                sums_v[0, h : h + 1, :] = jnp.sum(scaled * mixing, axis=0, keepdims=True)
                col = jnp.sum(grad_mixing * mixing, axis=1, keepdims=True)
                sums = jnp.where(lane == h, col, sums)
            gs[b, :, cols] = jnp.where(low, halves[0], halves[1])
        rows = slice(b * HH, (b + 1) * HH)
        w_a = columns(remain[rows] * step[rows], growth[rows])
        w_b = columns(step[rows], step[rows])
        for k in range(W // 256):
            cols = slice(k * 256, (k + 1) * 256)
            remain_w = spread(w_a, 0, k)
            wide[1, b, :, cols] = remain_w.astype(BF)
            wide[2, b, :, cols] = (remain_w * x[:, cols].astype(F32)).astype(BF)
            wide[3, b, :, cols] = (spread(w_a, 1, k) * y[:, cols].astype(F32)).astype(BF)
            wide[0, b, :, cols] = (gs[b, :, cols] * spread(w_b, 0, k)).astype(BF)
        gs_bf = grad_scores.astype(BF)
        gb[b] = dot(gs_bf, cm[...])
        gc[b] = dot(grad_scores.T.astype(BF), bm[...])
    sums_v[1] = sums.T[: 2 * HH]


def block_decays(small, decay):
    for b in range(2):
        last = jnp.exp(small[2, b * HH : (b + 1) * HH, SPAN - 1 :])
        spread = jnp.where(iota((HH, W), 1) // HD == iota((HH, W), 0), last, 0.0)
        decay[b] = jnp.broadcast_to(jnp.sum(spread, axis=0, keepdims=True), (8, W))


def assemble(scal, got, keep, decay, start, end, exact):
    first = scal[1]
    second = 1 - first
    for k in range(W // 128):
        cols = slice(k * 128, (k + 1) * 128)
        d_first, d_second = decay[first, 0:1, cols], decay[second, 0:1, cols]
        for r in range(N // PIECE):
            at = k * (N // PIECE) + r
            rows = slice(r * PIECE, (r + 1) * PIECE)
            s_in, e_in = got[at, 0:PIECE, :], got[at, PIECE : 2 * PIECE, :]
            start[first, rows, cols] = s_in
            end[second, rows, cols] = e_in
            s_f, e_f = s_in.astype(F32), e_in.astype(F32)
            s_next = d_first * s_f + keep[0, rows, cols].astype(F32)
            e_next = d_second * e_f + keep[1, rows, cols].astype(F32)
            start[second, rows, cols] = s_next.astype(BF)
            end[first, rows, cols] = e_next.astype(BF)
            if exact is not None:
                one = jnp.sum(s_f * e_next, axis=0, keepdims=True)
                two = jnp.sum(s_next * e_f, axis=0, keepdims=True)
                if r == 0:
                    sum_one, sum_two = one, two
                else:
                    sum_one, sum_two = sum_one + one, sum_two + two
        if exact is not None:
            exact[first, 0:1, cols] = sum_one
            exact[second, 0:1, cols] = sum_two


def head_map(shape, head_dim, chan_dim):
    return jnp.where(iota(shape, chan_dim) // HD == iota(shape, head_dim), 1.0, 0.0).astype(BF)


def pre_kernel(
    scal, got, keep, small, sums_v, own, other, lo_in, lp_in,
    zed_own, zed_other, msg,
    start, end, exact, decay, rows_v, sems,
):
    late = copy_all(
        [(v, rows_v.at[pl.ds(SPAN * k, SPAN)]) for k, v in enumerate((lo_in, lp_in))], sems
    )
    block_decays(small, decay)
    assemble(scal, got, keep, decay, start, end, exact)
    by_head = head_map((W, 128), 1, 0)
    joint = []
    total = jnp.zeros((4 * SPAN, 128), F32)
    blocks = (parts_of(own), parts_of(other))
    for k in range(W // 256):
        cols = slice(k * 256, (k + 1) * 256)
        prods = []
        for b, (x, y, bm, cm) in enumerate(blocks):
            for grad, mat, state in ((x, bm, end), (y, cm, start)):
                prod = dot(mat[...], state[b, :, cols]) * grad[:, cols].astype(F32)
                prods.append(prod.astype(BF))
        total = total + dot(jnp.concatenate(prods, 0), by_head[cols])
    sums = [total[i * SPAN : (i + 1) * SPAN].T[:HH] for i in range(4)]
    for b in range(2):
        rows8 = jnp.concatenate(split3(exact[b, 0:1, :]) + [jnp.zeros((5, W), F32)], 0).astype(BF)
        joint.append(jnp.sum(dot_nt(head_map((HH, W), 0, 1), rows8), axis=1, keepdims=True))
    x_pulled = jnp.concatenate([sums[0], sums[2]], 0)
    y_state = jnp.concatenate([sums[1], sums[3]], 0)
    joint = jnp.concatenate(joint, 0)
    pre, step, cum = small[0], small[1], small[2]
    last = cum[:, SPAN - 1 :]
    rate = small[3]
    q = jnp.exp(last - cum) * x_pulled
    cols = sums_v[1]
    u = sums_v[0] - step * cols + jnp.exp(cum) * y_state
    grad_log = (
        sum_by(u, triangle(lambda u, t: u >= t))
        + sum_by(step * q, triangle(lambda u, t: u < t))
        + jnp.exp(last) * joint
    )
    grad_step = cols + q - rate * grad_log
    grad_pre = grad_step * jax.nn.sigmoid(pre)
    rolled = pltpu.roll(grad_pre, scal[2], 1)
    for k in range(TP):
        turn = rolled if k == 0 else pltpu.roll(rolled, 128 - 32 * k, 1)
        zed_own[k] = turn[:HH].astype(BF)
        zed_other[k] = turn[HH:].astype(BF)
    rolled = jnp.concatenate([rolled[:HH], rolled[HH:]], 1).astype(BF)
    diagonal = iota((HH, 128), 0) == iota((HH, 128), 1)

    def as_row(v):
        v = v[:HH] + v[HH:]
        v = jnp.sum(v, axis=1, keepdims=True)
        return jnp.sum(jnp.where(diagonal, v, 0.0), axis=0, keepdims=True)

    wait_all(late)
    extra = split3(as_row(grad_pre)) + split3(as_row(-grad_log * step))
    extra = jnp.concatenate(extra + [jnp.zeros((2, 128), F32)], 0)
    for k in range(D // 256):
        cols = slice(k * 256, (k + 1) * 256)
        part = dot(rolled, rows_v[:, cols])
        for j in range(2):
            whole = jnp.concatenate([part[:, j * 128 : (j + 1) * 128], extra], 0)
            msg[2 * k + j] = whole.astype(BF)


def sum_kernel(msg, out, totals):
    total = jnp.zeros((HH + 8, 128), F32)
    for k in range(CHIPS):
        total = total + msg[k].astype(F32)
    rounded = total[:HH].astype(BF)
    for k in range(CHIPS):
        out[k] = rounded
    e = total[HH:]
    bias = e[0:1] + e[1:2] + e[2:3]
    rate = e[3:4] + e[4:5] + e[5:6]
    totals[...] = jnp.concatenate([bias, rate, jnp.zeros((6, 128), F32)], 0)


def grads_kernel(
    scal, got, keep, small, wide_in, gb, gc, own, other,
    out_own, out_other,
    start, end, decay, wide, sems,
):
    loads = copy_all([(wide_in, wide)], sems)
    gs, remain, in_w, out_w = [wide.at[i] for i in range(4)]
    block_decays(small, decay)
    assemble(scal, got, keep, decay, start, end, None)
    wait_all(loads)
    for b, bm in enumerate((parts_of(own)[2], parts_of(other)[2])):
        grad_b, grad_c = gb[b], gc[b]
        out = (out_own, out_other)[b]
        for k in range(W // 256):
            cols = slice(k * 256, (k + 1) * 256)
            pulled = dot(bm[...], end[b, :, cols])
            out[:, cols] = (
                gs[b, :, cols].astype(F32) + remain[b, :, cols].astype(F32) * pulled
            ).astype(BF)
            grad_b = grad_b + dot_nt(in_w[b, :, cols], end[b, :, cols])
            grad_c = grad_c + dot_nt(out_w[b, :, cols], start[b, :, cols])
        out[:, W : W + N] = grad_b.astype(BF)
        out[:, W + N :] = grad_c.astype(BF)


def final_kernel(
    own, other, params, t_own, t_other, w_own, w_other, gx, gb, gc, g_bias, g_rate, g_weight
):
    at_zero = lax.axis_index("core") == 0

    def join(a, b):
        return jnp.where(at_zero, a, b), jnp.where(at_zero, b, a)

    for out, at, width in ((gx, 0, W), (gb, W, N), (gc, W + N, N)):
        cols = slice(at, at + width)
        out[:, :width], out[:, width:] = join(own[:, cols], other[:, cols])
    low, high = join(t_own[...], t_other[...])
    lane = iota((8, 128), 1)
    total = jnp.where(lane < HH, low, pltpu.roll(high, HH, 1))
    g_bias[...] = total[0:1, : 2 * HH]
    g_rate[...] = total[1:2, : 2 * HH] * jnp.exp(params[1:2])
    for j in range(CHIPS):
        cols = slice(j * 128, (j + 1) * 128)
        g_weight[0:HH, cols], g_weight[HH:, cols] = join(
            w_own[j].astype(F32), w_other[j].astype(F32)
        )


def turn_kernel(own, other, *outs):
    for k, out in enumerate(outs):
        out[:HH] = own[k]
        out[HH:] = other[k]


def input_kernel(scal, a0, a1, a2, a3, w0, w1, w2, w3, out, mat, sems):
    first = scal[1]
    copies = []
    for k, w in enumerate((w0, w1, w2, w3)):
        for j, side in enumerate((first, 1 - first)):
            part = w.at[pl.ds(pl.multiple_of(HH * side, HH), HH)]
            place = mat.at[pl.ds(2 * HH * k + HH * j, HH)]
            copies += copy_all([(part, place)], sems, 2 * k + j)
    rows = [a[...] for a in (a0, a1, a2, a3)]
    zed = jnp.concatenate(rows, 0).astype(F32).T[:32].astype(BF)
    wait_all(copies)
    for k in range(D // 512):
        cols = slice(k * 512, (k + 1) * 512)
        out[:, cols] = dot(zed, mat[:, cols]).astype(BF)


def call(kernel, outs, args, scratch=(), sems=0, far_in=(), far_out=(), flops=0, moved=0, limit=16):
    near = pl.BlockSpec(memory_space=pltpu.VMEM)
    far = pl.BlockSpec(memory_space=pltpu.HBM)
    specs = []
    for i, a in enumerate(args):
        if a.dtype == jnp.int32:
            specs.append(pl.BlockSpec(memory_space=pltpu.SMEM))
        else:
            specs.append(far if i in far_in else near)
    shapes = [pltpu.VMEM(s, t) for s, t in scratch]
    if sems:
        shapes.append(pltpu.SemaphoreType.DMA((sems,)))
    return pl.pallas_call(
        kernel,
        out_shape=[jax.ShapeDtypeStruct(s, t) for s, t in outs],
        in_specs=specs,
        out_specs=[far if i in far_out else near for i in range(len(outs))],
        scratch_shapes=shapes,
        compiler_params=pltpu.CompilerParams(vmem_limit_bytes=int(limit * 2**20)),
        cost_estimate=pl.CostEstimate(flops=flops, bytes_accessed=moved, transcendentals=0),
    )(*args)


def swap(v):
    return lax.ppermute(v, "core", [(0, 1), (1, 0)])


def round_tp(v, k):
    return lax.ppermute(v, "tp", [(i, (i + k) % TP) for i in range(TP)])


def local(layer_input, dt_weight, dt_bias, a_log, ssm_input, b_in, c_in, out_grad):
    core = lax.axis_index("core")
    tp = lax.axis_index("tp")
    scal = jnp.stack([32 * tp, core, (128 - 32 * tp) % 128]).astype(jnp.int32)

    def half(v, which, width, axis):
        return lax.dynamic_slice_in_dim(v, which * width, width, axis)

    pieces = [layer_input] + [
        lax.ppermute(layer_input, "tp", [((i + k) % TP, i) for i in range(TP)]) for k in (1, 3, 2)
    ]
    pieces = [pieces[0], pieces[1], pieces[3], pieces[2]]
    weight_t = dt_weight.T
    weight_mine = jnp.concatenate(
        [half(weight_t, core, HH, 0), half(weight_t, 1 - core, HH, 0)], 0
    )
    pack_t = ((SPAN, 2 * W + 2 * N), BF)
    mine, theirs = call(pack_kernel, [pack_t] * 2, [scal, ssm_input, out_grad, b_in, c_in])
    operands = [mine, swap(theirs)]
    params = jnp.stack([dt_bias, a_log])
    small_t = ((4, 2 * HH, 128), F32)
    keep_t = ((2, N, W), BF)

    proj_own, proj_other = call(
        project_kernel,
        [((2, HH, 128), F32), ((HH, 128), F32)],
        [scal, weight_mine, params] + pieces[::-1],
        limit=16,
        flops=2**26,
        moved=2**21,
    )
    proj_other = swap(proj_other)
    msg_t = ((CHIPS, 2 * PIECE + 8, 128), BF)
    msg, keep, small = call(
        state_kernel,
        [msg_t, keep_t, small_t],
        [scal, proj_own, proj_other] + operands,
        [((2, N, W), F32), ((2, N, W), F32), ((2, 8, W), F32)],
        limit=STATE_LIMIT,
        flops=2**28,
        moved=2**22,
    )
    got = lax.all_to_all(msg, "chip", 0, 0, tiled=True)

    weight_t, small = lax.optimization_barrier((weight_t, small))
    near = [round_tp(weight_t, k) for k in (1, 3)]
    far = round_tp(weight_t, 2)
    rows_own = jnp.concatenate(pieces, 0)
    rows_other = swap(rows_own)
    sums_t = ((2, 2 * HH, 128), F32)
    wide_t = ((4, 2, SPAN, W), BF)
    wide, gb, gc, sums = call(
        intra_kernel,
        [wide_t, ((2, SPAN, N), F32), ((2, SPAN, N), F32), sums_t],
        [small] + operands,
        [((2, SPAN, W), F32)],
        limit=INTRA_LIMIT,
    )

    got, near = lax.optimization_barrier((got, near))
    (folded,) = call(
        fold_kernel, [((CHIPS, 2 * PIECE, 128), BF)], [got], flops=2**20, moved=2**20, limit=16
    )
    states = lax.all_to_all(folded, "chip", 0, 0, tiled=True)
    states, far = lax.optimization_barrier((states, far))
    weights = [weight_t, near[0], far, near[1]]

    parts_t = ((CHIPS, HH + 8, 128), BF)
    state_scratch = [((2, N, W), BF), ((2, N, W), BF)]
    zed_own, zed_other, parts = call(
        pre_kernel,
        [((TP, HH, 128), BF)] * 2 + [parts_t],
        [scal, states, keep, small, sums] + operands + [rows_own, rows_other],
        state_scratch
        + [((2, 8, W), F32), ((2, 8, W), F32), ((2 * SPAN, D), BF)],
        sems=2,
        far_in=(7, 8),
        flops=2**29,
        moved=2**23,
        limit=PRE_LIMIT,
    )
    shares = lax.all_to_all(parts, "chip", 0, 0, tiled=True)

    out_t = ((SPAN, W + 2 * N), BF)
    out_own, out_other = call(
        grads_kernel,
        [out_t] * 2,
        [scal, states, keep, small, wide, gb, gc] + operands,
        state_scratch + [((2, 8, W), F32), wide_t],
        sems=1,
        far_in=(4,),
        limit=GRADS_LIMIT,
    )
    out_other = swap(out_other)
    zed = call(turn_kernel, [((2 * HH, 128), BF)] * TP, [zed_own, swap(zed_other)])
    shares, zed, out_own, out_other = lax.optimization_barrier((shares, zed, out_own, out_other))
    total, totals = call(
        sum_kernel, [((CHIPS, HH, 128), BF), ((8, 128), F32)], [shares], flops=2**20, moved=2**20, limit=16
    )
    weight_own = lax.all_to_all(total, "chip", 0, 0, tiled=True)

    zed, total = lax.optimization_barrier((zed, total))
    zed = [zed[0]] + [round_tp(zed[k], k) for k in (1, 2, 3)]
    (grad_layer_input,) = call(
        input_kernel,
        [((32, D), BF)],
        [scal] + zed + weights,
        [((TP * 2 * HH, D), BF)],
        sems=8,
        far_in=(5, 6, 7, 8),
        limit=INPUT_LIMIT,
    )

    weight_own, grad_layer_input, totals_other = lax.optimization_barrier(
        (weight_own, grad_layer_input, swap(totals))
    )
    grad_ssm_input, grad_b_in, grad_c_in, grad_dt_bias, grad_a_log, grad_dt_weight = call(
        final_kernel,
        [((SPAN, 2 * W), BF), ((SPAN, 2 * N), BF), ((SPAN, 2 * N), BF)]
        + [((1, 2 * HH), F32)] * 2
        + [((2 * HH, D), F32)],
        [out_own, out_other, params, totals, totals_other, weight_own, swap(weight_own)],
    )
    return (
        grad_ssm_input,
        grad_b_in,
        grad_c_in,
        grad_layer_input,
        grad_dt_weight.T,
        grad_dt_bias[0],
        grad_a_log[0],
    )


def solution(mesh):
    fine = Mesh(mesh.devices.reshape(CHIPS, CORES, TP), ("chip", "core", "tp"))
    ctx = ("chip", "core")
    everything = ("chip", "core", "tp")
    placed = (
        P(everything, None),
        P(None, "tp"),
        P("tp"),
        P("tp"),
        P(ctx, "tp"),
        P(ctx, "tp"),
        P(ctx, "tp"),
        P(ctx, "tp"),
    )
    return jax.shard_map(
        local,
        mesh=fine,
        in_specs=placed,
        out_specs=(
            P(ctx, "tp"),
            P(ctx, "tp"),
            P(ctx, "tp"),
            P(everything, None),
            P(None, "tp"),
            P("tp"),
            P("tp"),
        ),
        check_vma=False,
    )
```

```python
import jax
import jax.numpy as jnp
from jax import lax
from jax.experimental import pallas as pl
from jax.experimental.pallas import tpu as pltpu
from jax.sharding import Mesh
from jax.sharding import PartitionSpec as P

LIMITS = 16, 16, 16, 16, 60
STATE_LIMIT, INTRA_LIMIT, PRE_LIMIT, GRADS_LIMIT, INPUT_LIMIT = LIMITS
BF = jnp.bfloat16
F32 = jnp.float32
CHIPS, CORES, TP = 32, 2, 4
SPAN = 128
N = 128
HD = 64
HH = 16
W = HH * HD
D = 4096
PIECE = 32


def dot(a, b):
    return lax.dot_general(a, b, (((1,), (0,)), ((), ())), preferred_element_type=F32)


def dot_nt(a, b):
    return lax.dot_general(a, b, (((1,), (1,)), ((), ())), preferred_element_type=F32)


def split3(v):
    hi = v.astype(BF).astype(F32)
    rest = v - hi
    mid = rest.astype(BF).astype(F32)
    return [hi, mid, rest - mid]


def iota(shape, dim):
    return lax.broadcasted_iota(jnp.int32, shape, dim)


def triangle(keep):
    return jnp.where(keep(iota((SPAN, SPAN), 0), iota((SPAN, SPAN), 1)), 1.0, 0.0).astype(BF)


def sum_by(rows, matrix):
    r = rows.shape[0]
    out = dot(jnp.concatenate(split3(rows), 0).astype(BF), matrix)
    return out[:r] + out[r : 2 * r] + out[2 * r :]


def columns(first, second):
    stack = split3(first) + split3(second) + [jnp.zeros((32, SPAN), F32)]
    return jnp.concatenate(stack, 0).T.astype(BF)


def spreader():
    row = iota((128, 256), 0)
    off = row % HH - iota((128, 256), 1) // HD
    offs = [jnp.where(row // 48 == part, off, -99) for part in range(2)]

    def spread(cols, part, k):
        return dot(cols, jnp.where(offs[part] == 4 * k, 1.0, 0.0).astype(BF))

    return spread


def copy_all(pairs, sems, first=0):
    copies = [pltpu.make_async_copy(a, b, sems.at[first + i]) for i, (a, b) in enumerate(pairs)]
    for c in copies:
        c.start()
    return copies


def wait_all(copies):
    for c in copies:
        c.wait()


def parts_of(pack):
    views = []
    for at, width in ((0, W), (W, W), (2 * W, N), (2 * W + N, N)):
        views.append(pack.at[:, pl.ds(at, width)])
    return views


def pack_kernel(scal, x, y, bm, cm, mine, theirs):
    first = scal[1]
    for out, side in ((mine, first), (theirs, 1 - first)):
        at = 0
        for v, width in ((x, W), (y, W), (bm, N), (cm, N)):
            place = pl.ds(pl.multiple_of(side * width, width), width)
            out[:, at : at + width] = v[:, place]
            at += width


def project_kernel(scal, w, params, l2, l3, l1, l0, own, other):
    first = scal[1]
    head = iota((2 * HH, 2 * HH), 0)
    head = jnp.where(first == 0, head, lax.rem(head + HH, 2 * HH))
    mine = iota((2 * HH, 2 * HH), 1) == head
    add = jnp.sum(jnp.where(mine, params[0:1], 0.0), axis=1, keepdims=True)
    rate = jnp.exp(jnp.sum(jnp.where(mine, params[1:2], 0.0), axis=1, keepdims=True))
    own[1] = jnp.broadcast_to(rate[:HH], (HH, 128))
    rows = jnp.concatenate([l0[...], l1[...], l2[...], l3[...]], 0)
    acc = pltpu.roll(dot_nt(w[...], rows), scal[0], 1) + add
    own[0] = acc[:HH]
    other[...] = acc[HH:]


def state_kernel(
    scal, po, pp, own, other,
    msg, keep, small,
    s_all, p_all, decay,
):
    first = scal[1]
    second = 1 - first
    pre = jnp.concatenate([po[0], pp[...]], 0)
    step = jnp.maximum(pre, 0.0) + jnp.log1p(jnp.exp(-jnp.abs(pre)))
    rate = jnp.concatenate([po[1], po[1]], 0)
    cum = sum_by(-rate * step, triangle(lambda u, t: u <= t))
    small[0] = pre
    small[1] = step
    small[2] = cum
    small[3] = rate
    spread = spreader()
    remain_step = jnp.exp(cum[:, SPAN - 1 :] - cum) * step
    growth = jnp.exp(cum)
    weights = [columns(remain_step[i : i + HH], growth[i : i + HH]) for i in (0, HH)]
    weights = jnp.concatenate(weights, 0)
    blocks = (parts_of(own), parts_of(other))
    mats = [[v[...].astype(F32).T.astype(BF) for v in block[2:]] for block in blocks]
    for k in range(W // 256):
        cols = slice(k * 256, (k + 1) * 256)
        w_in, w_out = spread(weights, 0, k), spread(weights, 1, k)
        for b, (x, y, _, _) in enumerate(blocks):
            rows = slice(b * SPAN, (b + 1) * SPAN)
            x_w = (w_in[rows] * x[:, cols].astype(F32)).astype(BF)
            y_w = (w_out[rows] * y[:, cols].astype(F32)).astype(BF)
            s_all[b, :, cols] = dot(mats[b][0], x_w)
            p_all[b, :, cols] = dot(mats[b][1], y_w)
            last = (b + 1) * SPAN - 1
            decay[b, :, cols] = jnp.broadcast_to(w_out[last : last + 1], (8, 256))
    per = N // PIECE
    for k in range(W // 128):
        cols = slice(k * 128, (k + 1) * 128)
        d_first, d_second = decay[first, 0:1, cols], decay[second, 0:1, cols]
        s_f, p_s = s_all[first, :, cols], p_all[second, :, cols]
        forward = d_second * s_f + s_all[second, :, cols]
        backward = p_all[first, :, cols] + d_first * p_s
        keep[0, :, cols] = s_f.astype(BF)
        keep[1, :, cols] = p_s.astype(BF)
        d3 = split3(d_first * d_second) + [jnp.zeros((5, 128), F32)]
        for r in range(per):
            rows = slice(r * PIECE, (r + 1) * PIECE)
            whole = jnp.concatenate([forward[rows], backward[rows]] + d3, 0)
            msg[k * per + r] = whole.astype(BF)


def fold_kernel(msg, out):
    parts = [msg[k].astype(F32) for k in range(CHIPS)]
    decays = [v[2 * PIECE : 2 * PIECE + 1] + v[2 * PIECE + 1 : 2 * PIECE + 2] + v[2 * PIECE + 2 : 2 * PIECE + 3] for v in parts]
    total = jnp.zeros((PIECE, 128), F32)
    for k in range(CHIPS):
        out[k, 0:PIECE, :] = total.astype(BF)
        total = total * decays[k] + parts[k][:PIECE]
    total = jnp.zeros((PIECE, 128), F32)
    for k in reversed(range(CHIPS)):
        out[k, PIECE : 2 * PIECE, :] = total.astype(BF)
        total = total * decays[k] + parts[k][PIECE : 2 * PIECE]


def intra_kernel(
    small, own, other,
    wide, gb, gc, sums_v,
    gs,
):
    spread = spreader()
    step, cum = small[1], small[2]
    remain = jnp.exp(cum[:, SPAN - 1 :] - cum)
    growth = jnp.exp(cum)
    lane = iota((SPAN, 128), 1)
    low = lane < HD
    later = lane >= iota((SPAN, SPAN), 0)
    step_t = jnp.concatenate([small[1], jnp.zeros((96, 128), F32)], 0).T
    cum_t = jnp.concatenate([small[2], jnp.zeros((96, 128), F32)], 0).T
    sums = jnp.zeros((SPAN, 128), F32)
    zero = jnp.zeros((SPAN, 128), BF)
    for b, (x, y, bm, cm) in enumerate((parts_of(own), parts_of(other))):
        scores = dot_nt(bm[...], cm[...])
        grad_scores = jnp.zeros((SPAN, SPAN), F32)
        for pair in range(HH // 2):
            cols = slice(pair * 128, (pair + 1) * 128)
            xs, ys = x[:, cols], y[:, cols]
            halves = []
            for side in range(2):
                h = b * HH + pair * 2 + side
                mine = jnp.where(low if side == 0 else ~low, xs, zero)
                grad_mixing = dot_nt(mine, ys)
                gap = small[2, h : h + 1, :] - cum_t[:, h : h + 1]
                decay = jnp.where(later, jnp.exp(jnp.minimum(gap, 0.0)), 0.0)
                mixing = scores * decay
                halves.append(dot(mixing.astype(BF), ys))
                scaled = grad_mixing * step_t[:, h : h + 1]
                grad_scores = grad_scores + scaled * decay
                sums_v[0, h : h + 1, :] = jnp.sum(scaled * mixing, axis=0, keepdims=True)
                col = jnp.sum(grad_mixing * mixing, axis=1, keepdims=True)
                sums = jnp.where(lane == h, col, sums)
            gs[b, :, cols] = jnp.where(low, halves[0], halves[1])
        rows = slice(b * HH, (b + 1) * HH)
        w_a = columns(remain[rows] * step[rows], growth[rows])
        w_b = columns(step[rows], step[rows])
        for k in range(W // 256):
            cols = slice(k * 256, (k + 1) * 256)
            remain_w = spread(w_a, 0, k)
            wide[1, b, :, cols] = remain_w.astype(BF)
            wide[2, b, :, cols] = (remain_w * x[:, cols].astype(F32)).astype(BF)
            wide[3, b, :, cols] = (spread(w_a, 1, k) * y[:, cols].astype(F32)).astype(BF)
            wide[0, b, :, cols] = (gs[b, :, cols] * spread(w_b, 0, k)).astype(BF)
        gs_bf = grad_scores.astype(BF)
        gb[b] = dot(gs_bf, cm[...])
        gc[b] = dot(grad_scores.T.astype(BF), bm[...])
    sums_v[1] = sums.T[: 2 * HH]


def block_decays(small, decay):
    for b in range(2):
        last = jnp.exp(small[2, b * HH : (b + 1) * HH, SPAN - 1 :])
        spread = jnp.where(iota((HH, W), 1) // HD == iota((HH, W), 0), last, 0.0)
        decay[b] = jnp.broadcast_to(jnp.sum(spread, axis=0, keepdims=True), (8, W))


def assemble(scal, got, keep, decay, start, end, exact):
    first = scal[1]
    second = 1 - first
    for k in range(W // 128):
        cols = slice(k * 128, (k + 1) * 128)
        d_first, d_second = decay[first, 0:1, cols], decay[second, 0:1, cols]
        for r in range(N // PIECE):
            at = k * (N // PIECE) + r
            rows = slice(r * PIECE, (r + 1) * PIECE)
            s_in, e_in = got[at, 0:PIECE, :], got[at, PIECE : 2 * PIECE, :]
            start[first, rows, cols] = s_in
            end[second, rows, cols] = e_in
            s_f, e_f = s_in.astype(F32), e_in.astype(F32)
            s_next = d_first * s_f + keep[0, rows, cols].astype(F32)
            e_next = d_second * e_f + keep[1, rows, cols].astype(F32)
            start[second, rows, cols] = s_next.astype(BF)
            end[first, rows, cols] = e_next.astype(BF)
            if exact is not None:
                one = jnp.sum(s_f * e_next, axis=0, keepdims=True)
                two = jnp.sum(s_next * e_f, axis=0, keepdims=True)
                if r == 0:
                    sum_one, sum_two = one, two
                else:
                    sum_one, sum_two = sum_one + one, sum_two + two
        if exact is not None:
            exact[first, 0:1, cols] = sum_one
            exact[second, 0:1, cols] = sum_two


def head_map(shape, head_dim, chan_dim):
    return jnp.where(iota(shape, chan_dim) // HD == iota(shape, head_dim), 1.0, 0.0).astype(BF)


def pre_kernel(
    scal, got, keep, small, sums_v, own, other, lo_in, lp_in,
    zed_own, zed_other, msg,
    start, end, exact, decay, rows_v, sems,
):
    late = copy_all(
        [(v, rows_v.at[pl.ds(SPAN * k, SPAN)]) for k, v in enumerate((lo_in, lp_in))], sems
    )
    block_decays(small, decay)
    assemble(scal, got, keep, decay, start, end, exact)
    by_head = head_map((W, 128), 1, 0)
    joint = []
    total = jnp.zeros((4 * SPAN, 128), F32)
    blocks = (parts_of(own), parts_of(other))
    for k in range(W // 256):
        cols = slice(k * 256, (k + 1) * 256)
        prods = []
        for b, (x, y, bm, cm) in enumerate(blocks):
            for grad, mat, state in ((x, bm, end), (y, cm, start)):
                prod = dot(mat[...], state[b, :, cols]) * grad[:, cols].astype(F32)
                prods.append(prod.astype(BF))
        total = total + dot(jnp.concatenate(prods, 0), by_head[cols])
    sums = [total[i * SPAN : (i + 1) * SPAN].T[:HH] for i in range(4)]
    for b in range(2):
        rows8 = jnp.concatenate(split3(exact[b, 0:1, :]) + [jnp.zeros((5, W), F32)], 0).astype(BF)
        joint.append(jnp.sum(dot_nt(head_map((HH, W), 0, 1), rows8), axis=1, keepdims=True))
    x_pulled = jnp.concatenate([sums[0], sums[2]], 0)
    y_state = jnp.concatenate([sums[1], sums[3]], 0)
    joint = jnp.concatenate(joint, 0)
    pre, step, cum = small[0], small[1], small[2]
    last = cum[:, SPAN - 1 :]
    rate = small[3]
    q = jnp.exp(last - cum) * x_pulled
    cols = sums_v[1]
    u = sums_v[0] - step * cols + jnp.exp(cum) * y_state
    grad_log = (
        sum_by(u, triangle(lambda u, t: u >= t))
        + sum_by(step * q, triangle(lambda u, t: u < t))
        + jnp.exp(last) * joint
    )
    grad_step = cols + q - rate * grad_log
    grad_pre = grad_step * jax.nn.sigmoid(pre)
    rolled = pltpu.roll(grad_pre, scal[2], 1)
    for k in range(TP):
        turn = rolled if k == 0 else pltpu.roll(rolled, 128 - 32 * k, 1)
        zed_own[k] = turn[:HH].astype(BF)
        zed_other[k] = turn[HH:].astype(BF)
    rolled = jnp.concatenate([rolled[:HH], rolled[HH:]], 1).astype(BF)
    diagonal = iota((HH, 128), 0) == iota((HH, 128), 1)

    def as_row(v):
        v = v[:HH] + v[HH:]
        v = jnp.sum(v, axis=1, keepdims=True)
        return jnp.sum(jnp.where(diagonal, v, 0.0), axis=0, keepdims=True)

    wait_all(late)
    extra = split3(as_row(grad_pre)) + split3(as_row(-grad_log * step))
    extra = jnp.concatenate(extra + [jnp.zeros((2, 128), F32)], 0)
    for k in range(D // 256):
        cols = slice(k * 256, (k + 1) * 256)
        part = dot(rolled, rows_v[:, cols])
        for j in range(2):
            whole = jnp.concatenate([part[:, j * 128 : (j + 1) * 128], extra], 0)
            msg[2 * k + j] = whole.astype(BF)


def sum_kernel(msg, out, totals):
    total = jnp.zeros((HH + 8, 128), F32)
    for k in range(CHIPS):
        total = total + msg[k].astype(F32)
    rounded = total[:HH].astype(BF)
    for k in range(CHIPS):
        out[k] = rounded
    e = total[HH:]
    bias = e[0:1] + e[1:2] + e[2:3]
    rate = e[3:4] + e[4:5] + e[5:6]
    totals[...] = jnp.concatenate([bias, rate, jnp.zeros((6, 128), F32)], 0)


def grads_kernel(
    scal, got, keep, small, wide_in, gb, gc, own, other,
    out_own, out_other,
    start, end, decay, wide, sems,
):
    loads = copy_all([(wide_in, wide)], sems)
    gs, remain, in_w, out_w = [wide.at[i] for i in range(4)]
    block_decays(small, decay)
    assemble(scal, got, keep, decay, start, end, None)
    wait_all(loads)
    for b, bm in enumerate((parts_of(own)[2], parts_of(other)[2])):
        grad_b, grad_c = gb[b], gc[b]
        out = (out_own, out_other)[b]
        for k in range(W // 256):
            cols = slice(k * 256, (k + 1) * 256)
            pulled = dot(bm[...], end[b, :, cols])
            out[:, cols] = (
                gs[b, :, cols].astype(F32) + remain[b, :, cols].astype(F32) * pulled
            ).astype(BF)
            grad_b = grad_b + dot_nt(in_w[b, :, cols], end[b, :, cols])
            grad_c = grad_c + dot_nt(out_w[b, :, cols], start[b, :, cols])
        out[:, W : W + N] = grad_b.astype(BF)
        out[:, W + N :] = grad_c.astype(BF)


def final_kernel(
    own, other, params, t_own, t_other, w_own, w_other, gx, gb, gc, g_bias, g_rate, g_weight
):
    at_zero = lax.axis_index("core") == 0

    def join(a, b):
        return jnp.where(at_zero, a, b), jnp.where(at_zero, b, a)

    for out, at, width in ((gx, 0, W), (gb, W, N), (gc, W + N, N)):
        cols = slice(at, at + width)
        out[:, :width], out[:, width:] = join(own[:, cols], other[:, cols])
    low, high = join(t_own[...], t_other[...])
    lane = iota((8, 128), 1)
    total = jnp.where(lane < HH, low, pltpu.roll(high, HH, 1))
    g_bias[...] = total[0:1, : 2 * HH]
    g_rate[...] = total[1:2, : 2 * HH] * jnp.exp(params[1:2])
    for j in range(CHIPS):
        cols = slice(j * 128, (j + 1) * 128)
        g_weight[0:HH, cols], g_weight[HH:, cols] = join(
            w_own[j].astype(F32), w_other[j].astype(F32)
        )


def turn_kernel(own, other, *outs):
    for k, out in enumerate(outs):
        out[:HH] = own[k]
        out[HH:] = other[k]


def input_kernel(scal, a0, a1, a2, a3, w0, w1, w2, w3, out):
    first = scal[1]
    sides = [pl.ds(pl.multiple_of(HH * side, HH), HH) for side in (first, 1 - first)]
    rows = [a[...] for a in (a0, a1, a2, a3)]
    zed = jnp.concatenate(rows, 0).astype(F32).T[:32].astype(BF)
    for k in range(D // 512):
        cols = slice(k * 512, (k + 1) * 512)
        mat = [w[side, cols] for w in (w0, w1, w2, w3) for side in sides]
        out[:, cols] = dot(zed, jnp.concatenate(mat, 0)).astype(BF)


def call(kernel, outs, args, scratch=(), sems=0, far_in=(), far_out=(), flops=0, moved=0, limit=16):
    near = pl.BlockSpec(memory_space=pltpu.VMEM)
    far = pl.BlockSpec(memory_space=pltpu.HBM)
    specs = []
    for i, a in enumerate(args):
        if a.dtype == jnp.int32:
            specs.append(pl.BlockSpec(memory_space=pltpu.SMEM))
        else:
            specs.append(far if i in far_in else near)
    shapes = [pltpu.VMEM(s, t) for s, t in scratch]
    if sems:
        shapes.append(pltpu.SemaphoreType.DMA((sems,)))
    return pl.pallas_call(
        kernel,
        out_shape=[jax.ShapeDtypeStruct(s, t) for s, t in outs],
        in_specs=specs,
        out_specs=[far if i in far_out else near for i in range(len(outs))],
        scratch_shapes=shapes,
        compiler_params=pltpu.CompilerParams(vmem_limit_bytes=int(limit * 2**20)),
        cost_estimate=pl.CostEstimate(flops=flops, bytes_accessed=moved, transcendentals=0),
    )(*args)


def swap(v):
    return lax.ppermute(v, "core", [(0, 1), (1, 0)])


def round_tp(v, k):
    return lax.ppermute(v, "tp", [(i, (i + k) % TP) for i in range(TP)])


def local(layer_input, dt_weight, dt_bias, a_log, ssm_input, b_in, c_in, out_grad):
    core = lax.axis_index("core")
    tp = lax.axis_index("tp")
    scal = jnp.stack([32 * tp, core, (128 - 32 * tp) % 128]).astype(jnp.int32)

    def half(v, which, width, axis):
        return lax.dynamic_slice_in_dim(v, which * width, width, axis)

    pieces = [layer_input] + [
        lax.ppermute(layer_input, "tp", [((i + k) % TP, i) for i in range(TP)]) for k in (1, 3, 2)
    ]
    pieces = [pieces[0], pieces[1], pieces[3], pieces[2]]
    weight_t = dt_weight.T
    weight_mine = jnp.concatenate(
        [half(weight_t, core, HH, 0), half(weight_t, 1 - core, HH, 0)], 0
    )
    pack_t = ((SPAN, 2 * W + 2 * N), BF)
    mine, theirs = call(pack_kernel, [pack_t] * 2, [scal, ssm_input, out_grad, b_in, c_in])
    operands = [mine, swap(theirs)]
    params = jnp.stack([dt_bias, a_log])
    small_t = ((4, 2 * HH, 128), F32)
    keep_t = ((2, N, W), BF)

    proj_own, proj_other = call(
        project_kernel,
        [((2, HH, 128), F32), ((HH, 128), F32)],
        [scal, weight_mine, params] + [pieces[i] for i in (2, 3, 1, 0)],
        limit=16,
        flops=2**26,
        moved=2**21,
    )
    proj_other = swap(proj_other)
    msg_t = ((CHIPS, 2 * PIECE + 8, 128), BF)
    msg, keep, small = call(
        state_kernel,
        [msg_t, keep_t, small_t],
        [scal, proj_own, proj_other] + operands,
        [((2, N, W), F32), ((2, N, W), F32), ((2, 8, W), F32)],
        limit=STATE_LIMIT,
        flops=2**28,
        moved=2**22,
    )
    got = lax.all_to_all(msg, "chip", 0, 0, tiled=True)

    weight_t, small = lax.optimization_barrier((weight_t, small))
    near = [round_tp(weight_t, k) for k in (1, 3)]
    far = round_tp(weight_t, 2)
    rows_own = jnp.concatenate(pieces, 0)
    rows_other = swap(rows_own)
    sums_t = ((2, 2 * HH, 128), F32)
    wide_t = ((4, 2, SPAN, W), BF)
    wide, gb, gc, sums = call(
        intra_kernel,
        [wide_t, ((2, SPAN, N), F32), ((2, SPAN, N), F32), sums_t],
        [small] + operands,
        [((2, SPAN, W), F32)],
        limit=INTRA_LIMIT,
    )

    got, near = lax.optimization_barrier((got, near))
    (folded,) = call(
        fold_kernel, [((CHIPS, 2 * PIECE, 128), BF)], [got], flops=2**20, moved=2**20, limit=16
    )
    states = lax.all_to_all(folded, "chip", 0, 0, tiled=True)
    states, far = lax.optimization_barrier((states, far))
    weights = [weight_t, near[0], far, near[1]]

    parts_t = ((CHIPS, HH + 8, 128), BF)
    state_scratch = [((2, N, W), BF), ((2, N, W), BF)]
    zed_own, zed_other, parts = call(
        pre_kernel,
        [((TP, HH, 128), BF)] * 2 + [parts_t],
        [scal, states, keep, small, sums] + operands + [rows_own, rows_other],
        state_scratch
        + [((2, 8, W), F32), ((2, 8, W), F32), ((2 * SPAN, D), BF)],
        sems=2,
        far_in=(7, 8),
        flops=2**29,
        moved=2**23,
        limit=PRE_LIMIT,
    )
    shares = lax.all_to_all(parts, "chip", 0, 0, tiled=True)

    out_t = ((SPAN, W + 2 * N), BF)
    out_own, out_other = call(
        grads_kernel,
        [out_t] * 2,
        [scal, states, keep, small, wide, gb, gc] + operands,
        state_scratch + [((2, 8, W), F32), wide_t],
        sems=1,
        far_in=(4,),
        limit=GRADS_LIMIT,
    )
    out_other = swap(out_other)
    zed = call(turn_kernel, [((2 * HH, 128), BF)] * TP, [zed_own, swap(zed_other)])
    shares, zed, out_own, out_other = lax.optimization_barrier((shares, zed, out_own, out_other))
    total, totals = call(
        sum_kernel, [((CHIPS, HH, 128), BF), ((8, 128), F32)], [shares], flops=2**20, moved=2**20, limit=16
    )
    weight_own = lax.all_to_all(total, "chip", 0, 0, tiled=True)

    zed, total = lax.optimization_barrier((zed, total))
    zed = [zed[0]] + [round_tp(zed[k], k) for k in (1, 2, 3)]
    (grad_layer_input,) = call(
        input_kernel,
        [((32, D), BF)],
        [scal] + zed + weights,
        limit=INPUT_LIMIT,
    )

    weight_own, grad_layer_input, totals_other = lax.optimization_barrier(
        (weight_own, grad_layer_input, swap(totals))
    )
    grad_ssm_input, grad_b_in, grad_c_in, grad_dt_bias, grad_a_log, grad_dt_weight = call(
        final_kernel,
        [((SPAN, 2 * W), BF), ((SPAN, 2 * N), BF), ((SPAN, 2 * N), BF)]
        + [((1, 2 * HH), F32)] * 2
        + [((2 * HH, D), F32)],
        [out_own, out_other, params, totals, totals_other, weight_own, swap(weight_own)],
    )
    return (
        grad_ssm_input,
        grad_b_in,
        grad_c_in,
        grad_layer_input,
        grad_dt_weight.T,
        grad_dt_bias[0],
        grad_a_log[0],
    )


def solution(mesh):
    fine = Mesh(mesh.devices.reshape(CHIPS, CORES, TP), ("chip", "core", "tp"))
    ctx = ("chip", "core")
    everything = ("chip", "core", "tp")
    placed = (
        P(everything, None),
        P(None, "tp"),
        P("tp"),
        P("tp"),
        P(ctx, "tp"),
        P(ctx, "tp"),
        P(ctx, "tp"),
        P(ctx, "tp"),
    )
    return jax.shard_map(
        local,
        mesh=fine,
        in_specs=placed,
        out_specs=(
            P(ctx, "tp"),
            P(ctx, "tp"),
            P(ctx, "tp"),
            P(everything, None),
            P(None, "tp"),
            P("tp"),
            P("tp"),
        ),
        check_vma=False,
    )
```
